128 devices in a mesh: row: 8 (over x, core), col: 16 (over z, y).
Axes of the slice: x: 4, y: 4, z: 4, core: 2. Of those that a mesh axis runs over, the one named last changes fastest.
Arguments:
- matrix: float32 [12288, 24576], P('row', 'col'), may hold values from -6 to 6
- far_diag: float32 [8, 1536], P('row'), may hold values from -6 to 6
- vectors: float32 [24576, 128], P(('row', 'col'))
- factors: float32 [128, 128], replicated, may hold values from -0.5 to 0.5
Outputs:
- updated: float32 [12288, 24576], P('row', 'col')
- far_updated: float32 [8, 1536], P('row')
The draws below stay inside these ranges and needn't reach their ends.
All inputs are finite; a program needn't handle non-finite values.
Results may differ from the reference program's by a relative error of at most 0.0003.
Values sent between devices are 32-bit elements; how exact they have to be, the bound alone decides.
A program may use at most 128 MiB of HBM per device.

```python
import jax
import jax.numpy as jnp
from jax import lax

TILE = 1536
NB = 128
GRID = 16
HALF = 8
N = 24576


def draw_vectors(key, part):
    spread = (N * NB) ** (-0.25)
    return spread * jax.random.normal(key, (N, NB), jnp.float32)


def level_of(stream_key, dims, shards, low, high):
    def one(dim, parts):
        steps = jax.random.uniform(jax.random.fold_in(jax.random.fold_in(stream_key, 6), dim), (parts,), jnp.float32, low / len(shards), high / len(shards))
        return jnp.repeat(jnp.exp(steps), dims[dim] // parts).reshape((-1,) + (1,) * (len(dims) - dim - 1))

    level = one(*shards[0])
    for cut in shards[1:]:
        level = level * one(*cut)
    return level


def bell_draw(own_key, extent, deviation, most, split=(), dtype=jnp.bfloat16):
    drawn = jax.random.normal(own_key, extent, jnp.float32) * deviation
    if len(split) > 0:
        drawn = level_of(own_key, extent, split, -0.22, 0.18) * drawn
    return jnp.clip(drawn, min=-most, max=most).astype(dtype)


def setup_inputs(seed: int = 0) -> dict:
    seeds = jax.random.split(jax.random.key(seed), 5)
    matrix = bell_draw(seeds[0], (HALF * TILE, GRID * TILE), 1.0, 6.0, ((0, 8), (1, 16)), jnp.float32)
    far_diag = bell_draw(seeds[1], (HALF, TILE), 1.0, 6.0, ((0, 8),), jnp.float32)
    vectors = draw_vectors(jax.random.fold_in(seeds[4], 71), 0)
    factors = bell_draw(seeds[3], (NB, NB), NB ** -0.5, 0.5, (), jnp.float32)
    return dict(matrix=matrix, far_diag=far_diag, vectors=vectors, factors=factors)


def product(left, right):
    return jnp.dot(left, right, preferred_element_type=jnp.float32, precision=lax.Precision.HIGHEST)


def sym_pair(block, low_diag):
    lower_part = jnp.tril(block)
    lead_full = lower_part + jnp.tril(block, -1).T
    upper_part = jnp.triu(block, 1)
    other_full = upper_part + upper_part.T + jnp.diag(low_diag)
    return lead_full, other_full


def tile_pair(row_at, col_at):
    far_row = GRID - 1 - row_at
    if col_at < row_at:
        return row_at, col_at
    if col_at == row_at:
        return row_at, far_row
    return far_row, col_at - row_at - 1


def reference(matrix, far_diag, vectors, factors):
    def block(row_at, col_at):
        return matrix[row_at * TILE:(row_at + 1) * TILE, col_at * TILE:(col_at + 1) * TILE]

    def vpart(index):
        return vectors[index * TILE:(index + 1) * TILE]

    zparts = [jnp.zeros((TILE, NB), jnp.float32) for index in range(GRID)]
    for row_at in range(HALF):
        for col_at in range(GRID):
            lead, other = tile_pair(row_at, col_at)
            tile_now = block(row_at, col_at)
            if col_at == row_at:
                lead_full, other_full = sym_pair(tile_now, far_diag[row_at])
                zparts[lead] = zparts[lead] + product(lead_full, vpart(lead))
                zparts[other] = zparts[other] + product(other_full, vpart(other))
            else:
                zparts[lead] = zparts[lead] + product(tile_now, vpart(other))
                zparts[other] = zparts[other] + product(tile_now.T, vpart(lead))
    zvals = jnp.concatenate(zparts, axis=0)
    gram_sum = product(vectors.T, zvals)
    middle = product(product(factors.T, gram_sum), factors)
    wvals = product(zvals, factors) - 0.5 * product(vectors, middle)

    def wpart(index):
        return wvals[index * TILE:(index + 1) * TILE]

    def change(lead, other):
        left = jnp.concatenate([vpart(lead), wpart(lead)], axis=1)
        right = jnp.concatenate([wpart(other), vpart(other)], axis=1)
        return product(left, right.T)

    row_blocks = []
    far_rows = []
    for row_at in range(HALF):
        pieces = []
        for col_at in range(GRID):
            lead, other = tile_pair(row_at, col_at)
            tile_now = block(row_at, col_at)
            if col_at == row_at:
                lead_full, other_full = sym_pair(tile_now, far_diag[row_at])
                lead_new = lead_full - change(lead, lead)
                other_new = other_full - change(other, other)
                pieces.append(jnp.tril(lead_new) + jnp.triu(other_new, 1))
            else:
                pieces.append(tile_now - change(lead, other))
        row_blocks.append(jnp.concatenate(pieces, axis=1))
        far_row = GRID - 1 - row_at
        far_rows.append(far_diag[row_at] - 2.0 * jnp.sum(vpart(far_row) * wpart(far_row), axis=1))
    return jnp.concatenate(row_blocks, axis=0), jnp.stack(far_rows, axis=0)
```

```python
import functools

import jax
import jax.numpy as jnp
from jax import lax
from jax.experimental import pallas as pl
from jax.experimental.pallas import tpu as pltpu
from jax.sharding import PartitionSpec as P

TILE = 1536
NB = 128
GRID = 16
HALF = 8
ROWS = 8
COLS = 16
VPIECE = 192
ZPIECE = 96
MESH = pl.DeviceIdType.MESH
F32 = jnp.float32
BF16 = jnp.bfloat16


def dot(left, right):
    return lax.dot_general(left, right, (((1,), (0,)), ((), ())), preferred_element_type=F32)


def dot_exact(left, right, dims=((1,), (0,))):
    return lax.dot_general(
        left, right, (dims, ((), ())), preferred_element_type=F32, precision=lax.Precision.HIGHEST
    )


def halves(value):
    high = value.astype(BF16)
    low = (value - high.astype(F32)).astype(BF16)
    return high, low


def member(tile, m):
    far = GRID - 1 - tile
    near_row = jnp.where(m <= tile, tile, jnp.where(m < HALF, m, m - HALF))
    near_col = jnp.where(m <= tile, m, jnp.where(m < HALF, tile, m - HALF + tile + 1))
    near_slot = jnp.where(m <= tile, 0, 1)
    far_row = jnp.where(m >= far, far, m)
    far_col = jnp.where(m >= far, m, GRID - far + m)
    far_slot = jnp.where(m > far, 0, 1)
    near = tile < HALF
    return (
        jnp.where(near, near_row, far_row),
        jnp.where(near, near_col, far_col),
        jnp.where(near, near_slot, far_slot),
    )


def put(src, dst, send_sem, recv_sem, to_row, to_col, row, col):
    here = jnp.logical_and(to_row == row, to_col == col)

    @pl.when(here)
    def _():
        pltpu.make_async_copy(src, dst, recv_sem).start()

    @pl.when(jnp.logical_not(here))
    def _():
        pltpu.make_async_remote_copy(
            src_ref=src, dst_ref=dst, send_sem=send_sem, recv_sem=recv_sem,
            device_id=(to_row, to_col), device_id_type=MESH,
        ).start()


def sent(src, send_sem, to_row, to_col, row, col):
    here = jnp.logical_and(to_row == row, to_col == col)

    @pl.when(jnp.logical_not(here))
    def _():
        pltpu.make_async_remote_copy(
            src_ref=src, dst_ref=src, send_sem=send_sem, recv_sem=send_sem,
            device_id=(to_row, to_col), device_id_type=MESH,
        ).wait_send()


def arrived(ref, sem):
    pltpu.make_async_copy(ref, ref, sem).wait()


def exchange(
    mat, lowd, vec, fac, xl_out, xrt_out, xl1_out, xrt0_out, d_out,
    abuf, ahi, alo, sym, vbuf, vcat, vtc, z, parts, zsum, zf, vd,
    gpart, g1, g1s, g2, g2s, gf, dmine, xl, xrt, xl1, xrt0,
    a_sem, v_send, v_recv, vd_send, vd_recv, r_send, r_recv, g_send, g_recv,
    z_send, z_recv, d_send, d_recv, o_sem,
):
    row = lax.axis_index("row")
    col = lax.axis_index("col")
    diag = row == col
    plain = row != col
    other = jnp.where(col < row, col, jnp.where(diag, GRID - 1 - row, col - row - 1))
    home = jnp.where(other < HALF, other, GRID - 1 - other)

    def part_copy(k):
        return pltpu.make_async_copy(
            mat.at[pl.ds(k * 384, 384)], abuf.at[pl.ds(k * 384, 384)], a_sem.at[k]
        )

    for k in range(4):
        part_copy(k).start()

    me = row * COLS + col
    bar = pltpu.get_barrier_semaphore()

    def greet(j, carry):
        to = lax.rem(me + j, ROWS * COLS)
        pl.semaphore_signal(
            bar, inc=1, device_id=(to // COLS, lax.rem(to, COLS)), device_id_type=MESH
        )
        return carry

    lax.fori_loop(1, ROWS * COLS, greet, 0)
    pl.semaphore_wait(bar, ROWS * COLS - 1)

    vtile = 2 * row + col // 8
    vpiece = lax.rem(col, 8)

    def v_args(j):
        m = lax.rem(j + 2 * vpiece, 16)
        return member(vtile, m)

    def v_put(j, carry):
        to_row, to_col, slot = v_args(j)
        put(vec, vbuf.at[slot, pl.ds(vpiece * VPIECE, VPIECE)], v_send.at[j], v_recv.at[slot],
            to_row, to_col, row, col)
        return carry

    lax.fori_loop(0, 16, v_put, 0)

    vfar = GRID - 1 - vtile

    @pl.when(vtile >= HALF)
    def _():
        for k in range(2):
            put(vec.at[pl.ds(k * ZPIECE, ZPIECE)], vd, vd_send.at[k], vd_recv,
                vfar, 2 * vpiece + k, row, col)

    for k in range(4):
        part_copy(k).wait()

        def split(s, carry):
            rows = pl.ds(pl.multiple_of(k * 384 + s * 32, 32), 32)
            high, low = halves(abuf[rows, :])
            ahi[rows, :] = high
            alo[rows, :] = low
            return carry

        lax.fori_loop(0, 12, split, 0)

    @pl.when(diag)
    def _():
        rr = lax.broadcasted_iota(jnp.int32, (256, 256), 0)
        cc = lax.broadcasted_iota(jnp.int32, (256, 256), 1)
        for p in range(6):
            at = slice(p * 256, p * 256 + 256)
            block = abuf[at, at]
            lower = jnp.where(rr > cc, block, 0.0)
            upper = jnp.where(rr < cc, block, 0.0)
            onto = jnp.where(rr == cc, block, 0.0)
            far_onto = jnp.where(rr == cc, jnp.broadcast_to(lowd[:, at], (256, 256)), 0.0)
            for s, full in ((0, lower + lower.T + onto), (1, upper + upper.T + far_onto)):
                high, low = halves(full)
                sym[s, 0, p] = high
                sym[s, 1, p] = low

    def cat_v(s):
        for p in range(6):
            at = slice(p * 256, p * 256 + 256)
            high, low = halves(vbuf[s, at, :])
            vcat[s, at, 0:128] = high
            vcat[s, at, 128:256] = low

    def cat_vt(s):
        for p in range(6):
            at = slice(p * 256, p * 256 + 256)
            high, low = halves(vbuf[s, at, :].T)
            vtc[s, 0:128, at] = high
            vtc[s, 128:256, at] = low

    def times(high, low, v):
        full = dot(high, v)
        return full[:, 0:128] + full[:, 128:256] + dot(low, v[:, 0:128])

    def times_t(vt, high, low):
        full = dot(vt, high)
        return full[0:128] + full[128:256] + dot(vt[0:128], low)

    def z_args(s, c):
        slot_m = jnp.where(col < row, row, jnp.where(
            diag, col, jnp.where(other < HALF, HALF + row, row)))
        if s == 0:
            to_row = row
            half = jnp.where(col <= row, 0, 1)
            m = col
        else:
            to_row = home
            half = jnp.where(other < HALF, 0, 1)
            m = slot_m
        return to_row, half * 16 + m

    def z_put(s, c):
        to_row, at = z_args(s, c)
        put(z.at[s, pl.ds(c * ZPIECE, ZPIECE)], parts.at[at], r_send.at[s, c], r_recv,
            to_row, c, row, col)

    def z_put_range(s, first, count):
        def one(j, carry):
            z_put(s, first + lax.rem(j + col, count))
            return carry

        lax.fori_loop(0, count, one, 0)

    def gram(s):
        high, low = halves(z[s])
        full = dot(vtc[s], high)
        return full[0:128] + full[128:256] + dot(vtc[s, 0:128, :], low)

    def g_start():
        def one(j, carry):
            c = lax.rem(j + col, COLS)
            put(gpart.at[pl.ds(pl.multiple_of(c * 8, 8), 8)], g1.at[col], g_send.at[0, c],
                g_recv.at[0], row, c, row, col)
            return carry

        lax.fori_loop(0, COLS, one, 0)

    arrived(vbuf.at[1], v_recv.at[1])
    cat_v(1)

    @pl.when(plain)
    def _():
        def panel(k, carry):
            rows = pl.ds(pl.multiple_of(k * 384, 384), 384)
            z[0, rows, :] = times(ahi[rows, :], alo[rows, :], vcat[1])
            z_put_range(0, k * 4, 4)
            return carry

        lax.fori_loop(0, 4, panel, 0)

    arrived(vbuf.at[0], v_recv.at[0])
    cat_vt(0)

    @pl.when(plain)
    def _():
        y = gram(0)
        gpart[...] = y + y.T
        g_start()

        def panel(k, carry):
            at = pl.ds(pl.multiple_of(k * 768, 768), 768)
            part = times_t(vtc[0], ahi[:, at], alo[:, at])
            z[1, at, :] = part.T
            z_put_range(1, k * 8, 8)
            return carry

        lax.fori_loop(0, 2, panel, 0)

    @pl.when(diag)
    def _():
        cat_v(0)
        cat_vt(1)
        for p in range(6):
            lo, hi = p * 256, p * 256 + 256
            at = slice(lo, hi)
            z0 = times(sym[0, 0, p], sym[0, 1, p], vcat[0, at, :])
            z1 = times(sym[1, 0, p], sym[1, 1, p], vcat[1, at, :])
            if p > 0:
                z0 += times(ahi[at, 0:lo], alo[at, 0:lo], vcat[0, 0:lo, :])
                z1 += times_t(vtc[1, :, 0:lo], ahi[0:lo, at], alo[0:lo, at]).T
            if p < 5:
                z1 += times(ahi[at, hi:], alo[at, hi:], vcat[1, hi:, :])
                z0 += times_t(vtc[0, :, hi:], ahi[hi:, at], alo[hi:, at]).T
            z[0, at, :] = z0
            z[1, at, :] = z1
        z_put_range(0, 0, 16)
        z_put_range(1, 0, 16)
        gpart[...] = gram(0) + gram(1)
        g_start()

    arrived(g1, g_recv.at[0])
    g1s[...] = jnp.sum(g1[...], axis=0)

    def g_line(j, carry):
        r = lax.rem(j + row, ROWS)
        put(g1s, g2.at[row], g_send.at[1, r], g_recv.at[1], r, col, row, col)
        return carry

    lax.fori_loop(0, ROWS, g_line, 0)
    arrived(g2, g_recv.at[1])
    g2s[...] = jnp.sum(g2[...], axis=0)

    def g_row(j, carry):
        c = lax.rem(j + col, COLS)
        put(g2s, gf.at[pl.ds(pl.multiple_of(col * 8, 8), 8)], g_send.at[2, c], g_recv.at[2],
            row, c, row, col)
        return carry

    lax.fori_loop(0, COLS, g_row, 0)

    arrived(parts, r_recv)
    zsum[0] = jnp.sum(parts[0:16], axis=0)
    zsum[1] = jnp.sum(parts[16:32], axis=0)

    def zf_args(j, half):
        tile = row if half == 0 else GRID - 1 - row
        return member(tile, lax.rem(j + col, 16))

    def zf_put(j, carry):
        for half in range(2):
            to_row, to_col, slot = zf_args(j, half)
            put(zsum.at[half], zf.at[slot, pl.ds(col * ZPIECE, ZPIECE)], z_send.at[half, j],
                z_recv.at[slot], to_row, to_col, row, col)
        return carry

    lax.fori_loop(0, 16, zf_put, 0)

    arrived(gf, g_recv.at[2])
    fac_value = fac[...]
    middle = dot_exact(dot_exact(fac_value, gf[...], ((0,), (0,))), fac_value)

    arrived(vd, vd_recv)
    v_far = vd[...]
    w_far = dot_exact(zsum[1], fac_value) - 0.5 * dot_exact(v_far, middle)
    sums = dot_exact(jnp.ones((8, 128), F32), v_far * w_far, ((1,), (1,)))
    dmine[...] = jnp.concatenate([sums, jnp.zeros((8, 32), F32)], axis=1)

    def d_put(j, carry):
        c = lax.rem(j + col, COLS)
        put(dmine, d_out.at[col], d_send.at[c], d_recv, row, c, row, col)
        return carry

    lax.fori_loop(0, COLS, d_put, 0)

    both = jnp.concatenate([fac_value, -0.5 * middle], axis=0)
    both_high, both_low = halves(both)
    both_t = both.T
    both_t_high, both_t_low = halves(both_t)

    def w_plain(s, out):
        def panel(k, carry):
            rows = pl.ds(pl.multiple_of(k * 256, 256), 256)
            v_high, v_low = halves(vbuf[s, rows, :])
            z_high, z_low = halves(zf[s, rows, :])
            high = jnp.concatenate([z_high, v_high], axis=1)
            low = jnp.concatenate([z_low, v_low], axis=1)
            w = dot(high, both_high) + dot(high, both_low) + dot(low, both_high)
            w_high, w_low = halves(w)
            out[rows, :] = jnp.concatenate([v_high, w_high, v_low, w_low], axis=1)
            return carry

        lax.fori_loop(0, 6, panel, 0)

    def w_turned(s, out):
        def panel(k, carry):
            rows = pl.ds(pl.multiple_of(k * 256, 256), 256)
            v_high, v_low = halves(vbuf[s, rows, :].T)
            z_high, z_low = halves(zf[s, rows, :].T)
            high = jnp.concatenate([z_high, v_high], axis=0)
            low = jnp.concatenate([z_low, v_low], axis=0)
            w = dot(both_t_high, high) + dot(both_t_low, high) + dot(both_t_high, low)
            w_high, w_low = halves(w)
            out[:, rows] = jnp.concatenate([w_high, v_high, w_low, v_low], axis=0)
            return carry

        lax.fori_loop(0, 6, panel, 0)

    arrived(zf.at[1], z_recv.at[1])
    w_turned(1, xrt)
    pltpu.make_async_copy(xrt, xrt_out, o_sem.at[0]).start()
    arrived(zf.at[0], z_recv.at[0])
    w_plain(0, xl)
    pltpu.make_async_copy(xl, xl_out, o_sem.at[1]).start()

    @pl.when(diag)
    def _():
        w_plain(1, xl1)
        w_turned(0, xrt0)
        pltpu.make_async_copy(xl1, xl1_out, o_sem.at[2]).start()
        pltpu.make_async_copy(xrt0, xrt0_out, o_sem.at[3]).start()

    arrived(d_out, d_recv)

    def all_sent(j, carry):
        to_row, to_col, slot = v_args(j)
        sent(vec, v_send.at[j], to_row, to_col, row, col)
        for s in range(2):
            to_row, at = z_args(s, j)
            sent(z.at[s, pl.ds(0, ZPIECE)], r_send.at[s, j], to_row, j, row, col)
            to_row, to_col, slot = zf_args(j, s)
            sent(zsum.at[s], z_send.at[s, j], to_row, to_col, row, col)
        sent(g1s, g_send.at[0, j], row, j, row, col)
        sent(g2s, g_send.at[2, j], row, j, row, col)
        sent(dmine, d_send.at[j], row, j, row, col)
        return carry

    lax.fori_loop(0, 16, all_sent, 0)

    def line_sent(j, carry):
        sent(g1s, g_send.at[1, j], j, col, row, col)
        return carry

    lax.fori_loop(0, ROWS, line_sent, 0)

    @pl.when(vtile >= HALF)
    def _():
        for k in range(2):
            sent(vd, vd_send.at[k], vfar, 2 * vpiece + k, row, col)

    arrived(xrt, o_sem.at[0])
    arrived(xl, o_sem.at[1])

    @pl.when(diag)
    def _():
        arrived(xl1, o_sem.at[2])
        arrived(xrt0, o_sem.at[3])


def update(mat, xl, xrt, d, fard, xl1_hbm, xrt0_hbm, out, far_out, xl1, xrt0, sem):
    step = pl.program_id(0)
    diag = lax.axis_index("row") == lax.axis_index("col")

    @pl.when(jnp.logical_and(diag, step == 0))
    def _():
        first = pltpu.make_async_copy(xl1_hbm, xl1, sem.at[0])
        second = pltpu.make_async_copy(xrt0_hbm, xrt0, sem.at[1])
        first.start()
        second.start()
        first.wait()
        second.wait()

    @pl.when(step == 0)
    def _():
        lane = lax.broadcasted_iota(jnp.int32, (128, TILE), 1)
        start = jnp.zeros((128, TILE), jnp.int32)
        for k in range(1, 16):
            start += jnp.where(lane >= k * ZPIECE, ZPIECE, 0)
        pick = jnp.where(lane - start == lax.broadcasted_iota(jnp.int32, (128, TILE), 0), 1.0, 0.0)
        spread = dot_exact(d[:, 0, :], pick)
        piece = lax.broadcasted_iota(jnp.int32, (16, TILE), 0) * ZPIECE
        whole = jnp.sum(jnp.where(piece == start[0:16], spread, 0.0), axis=0, keepdims=True)
        far_out[...] = fard[...] - 2.0 * whole

    def change(left, right):
        high, low = left[:, 0:256], left[:, 256:512]
        return dot(high, right[0:256]) + dot(high, right[256:512]) + dot(low, right[0:256])

    rows = pl.ds(pl.multiple_of(step * 256, 256), 256)

    @pl.when(jnp.logical_not(diag))
    def _():
        out[...] = mat[...] - change(xl[rows, :], xrt[...])

    @pl.when(diag)
    def _():
        lead = change(xl[rows, :], xrt0[...])
        far = change(xl1[rows, :], xrt[...])
        at_row = lax.broadcasted_iota(jnp.int32, (256, TILE), 0) + step * 256
        at_col = lax.broadcasted_iota(jnp.int32, (256, TILE), 1)
        out[...] = mat[...] - jnp.where(at_row >= at_col, lead, far)


def body(matrix, far_diag, vectors, factors):
    any_spec = pl.BlockSpec(memory_space=pl.ANY)
    vmem_spec = pl.BlockSpec(memory_space=pltpu.VMEM)
    dma = pltpu.SemaphoreType.DMA
    xl_shape = jax.ShapeDtypeStruct((TILE, 512), BF16)
    xrt_shape = jax.ShapeDtypeStruct((512, TILE), BF16)
    xl, xrt, xl1, xrt0, d = pl.pallas_call(
        exchange,
        name="exchange",
        out_shape=(xl_shape, xrt_shape, xl_shape, xrt_shape,
                   jax.ShapeDtypeStruct((16, 8, 128), F32)),
        in_specs=[any_spec, vmem_spec, vmem_spec, vmem_spec],
        out_specs=(any_spec, any_spec, any_spec, any_spec, vmem_spec),
        scratch_shapes=[
            pltpu.VMEM((TILE, TILE), F32),
            pltpu.VMEM((TILE, TILE), BF16),
            pltpu.VMEM((TILE, TILE), BF16),
            pltpu.VMEM((2, 2, 6, 256, 256), BF16),
            pltpu.VMEM((2, TILE, NB), F32),
            pltpu.VMEM((2, TILE, 2 * NB), BF16),
            pltpu.VMEM((2, 2 * NB, TILE), BF16),
            pltpu.VMEM((2, TILE, NB), F32),
            pltpu.VMEM((32, ZPIECE, NB), F32),
            pltpu.VMEM((2, ZPIECE, NB), F32),
            pltpu.VMEM((2, TILE, NB), F32),
            pltpu.VMEM((ZPIECE, NB), F32),
            pltpu.VMEM((NB, NB), F32),
            pltpu.VMEM((16, 8, NB), F32),
            pltpu.VMEM((8, NB), F32),
            pltpu.VMEM((8, 8, NB), F32),
            pltpu.VMEM((8, NB), F32),
            pltpu.VMEM((NB, NB), F32),
            pltpu.VMEM((8, NB), F32),
            pltpu.VMEM((TILE, 512), BF16),
            pltpu.VMEM((512, TILE), BF16),
            pltpu.VMEM((TILE, 512), BF16),
            pltpu.VMEM((512, TILE), BF16),
            dma((4,)),
            dma((16,)),
            dma((2,)),
            dma((2,)),
            dma,
            dma((2, 16)),
            dma,
            dma((3, 16)),
            dma((3,)),
            dma((2, 16)),
            dma((2,)),
            dma((16,)),
            dma,
            dma((4,)),
        ],
        compiler_params=pltpu.CompilerParams(
            collective_id=0, has_side_effects=True, vmem_limit_bytes=56 * 2**20
        ),
    )(matrix, far_diag, vectors, factors)
    whole = lambda *shape: pl.BlockSpec(shape, lambda i: (0,) * len(shape))
    updated, far_updated = pl.pallas_call(
        update,
        name="update",
        grid=(6,),
        out_shape=(jax.ShapeDtypeStruct((TILE, TILE), F32), jax.ShapeDtypeStruct((1, TILE), F32)),
        in_specs=[
            pl.BlockSpec((256, TILE), lambda i: (i, 0)),
            whole(TILE, 512),
            whole(512, TILE),
            whole(16, 8, 128),
            whole(1, TILE),
            any_spec,
            any_spec,
        ],
        out_specs=(pl.BlockSpec((256, TILE), lambda i: (i, 0)), whole(1, TILE)),
        scratch_shapes=[
            pltpu.VMEM((TILE, 512), BF16),
            pltpu.VMEM((512, TILE), BF16),
            dma((2,)),
        ],
        compiler_params=pltpu.CompilerParams(vmem_limit_bytes=48 * 2**20),
    )(matrix, xl, xrt, d, far_diag, xl1, xrt0)
    return updated, far_updated


def solution(mesh):
    in_specs = (P("row", "col"), P("row", None), P(("row", "col"), None), P())
    out_specs = (P("row", "col"), P("row", None))
    return jax.shard_map(body, mesh=mesh, in_specs=in_specs, out_specs=out_specs, check_vma=False)
```

```python
import functools

import jax
import jax.numpy as jnp
from jax import lax
from jax.experimental import pallas as pl
from jax.experimental.pallas import tpu as pltpu
from jax.sharding import PartitionSpec as P

TILE = 1536
NB = 128
GRID = 16
HALF = 8
ROWS = 8
LINE = ((0, 1), (1, 0), (3, 0), (1, 1), (3, 1), (2, 0), (2, 1))
COLS = 16
VPIECE = 192
ZPIECE = 96
MESH = pl.DeviceIdType.MESH
F32 = jnp.float32
BF16 = jnp.bfloat16


def dot(left, right):
    return lax.dot_general(left, right, (((1,), (0,)), ((), ())), preferred_element_type=F32)


def dot_exact(left, right, dims=((1,), (0,))):
    return lax.dot_general(
        left, right, (dims, ((), ())), preferred_element_type=F32, precision=lax.Precision.HIGHEST
    )


def halves(value):
    high = value.astype(BF16)
    low = (value - high.astype(F32)).astype(BF16)
    return high, low


def member(tile, m):
    far = GRID - 1 - tile
    near_row = jnp.where(m <= tile, tile, jnp.where(m < HALF, m, m - HALF))
    near_col = jnp.where(m <= tile, m, jnp.where(m < HALF, tile, m - HALF + tile + 1))
    near_slot = jnp.where(m <= tile, 0, 1)
    far_row = jnp.where(m >= far, far, m)
    far_col = jnp.where(m >= far, m, GRID - far + m)
    far_slot = jnp.where(m > far, 0, 1)
    near = tile < HALF
    return (
        jnp.where(near, near_row, far_row),
        jnp.where(near, near_col, far_col),
        jnp.where(near, near_slot, far_slot),
    )


def put(src, dst, send_sem, recv_sem, to_row, to_col, row, col):
    here = jnp.logical_and(to_row == row, to_col == col)

    @pl.when(here)
    def _():
        pltpu.make_async_copy(src, dst, recv_sem).start()

    @pl.when(jnp.logical_not(here))
    def _():
        pltpu.make_async_remote_copy(
            src_ref=src, dst_ref=dst, send_sem=send_sem, recv_sem=recv_sem,
            device_id=(to_row, to_col), device_id_type=MESH,
        ).start()


def sent(src, dst, send_sem, recv_sem, to_row, to_col, row, col):
    here = jnp.logical_and(to_row == row, to_col == col)

    @pl.when(jnp.logical_not(here))
    def _():
        pltpu.make_async_remote_copy(
            src_ref=src, dst_ref=src, send_sem=send_sem, recv_sem=send_sem,
            device_id=(to_row, to_col), device_id_type=MESH,
        ).wait_send()


def arrived(ref, sem):
    pltpu.make_async_copy(ref, ref, sem).wait()


def exchange(
    mat, lowd, vec, fac, xl_out, xrt_out, xl1_out, xrt0_out, d_out,
    abuf, ahi, alo, sym, vline, vbuf, vcat, vtc, z, parts, lpart, lsend, zsum, zf, vd,
    gpart, g1, g1s, g2, g2s, gf, dmine, xl, xrt, xl1, xrt0,
    a_sem, vl_send, vl_recv, vf_send, vo_send, v_recv, vd_send, vd_recv, r_send, r_recv,
    l_send, l_recv, g_send, g_recv, z_send, z_recv, d_send, d_recv, o_sem,
):
    row = lax.axis_index("row")
    col = lax.axis_index("col")
    diag = row == col
    plain = row != col
    other = jnp.where(col < row, col, jnp.where(diag, GRID - 1 - row, col - row - 1))
    far = GRID - 1 - row
    x, core = row // 2, lax.rem(row, 2)

    def line_row(step):
        return lax.rem(x + step[0], 4) * 2 + lax.rem(core + step[1], 2)

    def part_copy(k):
        return pltpu.make_async_copy(
            mat.at[pl.ds(k * 384, 384)], abuf.at[pl.ds(k * 384, 384)], a_sem.at[k]
        )

    for k in range(4):
        part_copy(k).start()

    bar = pltpu.get_barrier_semaphore()

    def greet(j, carry):
        pl.semaphore_signal(
            bar, inc=1, device_id=(row, lax.rem(col + j, COLS)), device_id_type=MESH
        )
        return carry

    lax.fori_loop(1, COLS, greet, 0)
    for step in LINE:
        pl.semaphore_signal(bar, inc=1, device_id=(line_row(step), col), device_id_type=MESH)

    own = pltpu.make_async_copy(vec, vline.at[row], vl_recv.at[row])
    own.start()

    def split_part(k):
        part_copy(k).wait()

        def split(s, carry):
            rows = pl.ds(pl.multiple_of(k * 384 + s * 32, 32), 32)
            high, low = halves(abuf[rows, :])
            ahi[rows, :] = high
            alo[rows, :] = low
            return carry

        lax.fori_loop(0, 12, split, 0)

    split_part(0)
    split_part(1)
    pl.semaphore_wait(bar, COLS - 1 + ROWS - 1)

    vtile = 2 * row + col // 8
    vpiece = lax.rem(col, 8)
    parity = col // 8
    vlead_row = jnp.where(vtile < HALF, vtile, GRID - 1 - vtile)

    def v_line(j, to_row):
        return pltpu.make_async_remote_copy(
            src_ref=vec, dst_ref=vline.at[row], send_sem=vl_send.at[j],
            recv_sem=vl_recv.at[row], device_id=(to_row, col), device_id_type=MESH,
        )

    def v_line_each(act):
        @pl.when(vlead_row != row)
        def _():
            act(v_line(7, vlead_row))

        for j, step in enumerate(LINE):
            to_row = line_row(step)

            @pl.when(jnp.logical_and(to_row != vlead_row, to_row <= GRID - 1 - vtile))
            def _():
                act(v_line(j, to_row))

    v_line_each(lambda copy: copy.start())

    lead_near = lax.rem(row, 2) == parity
    lead_src = jnp.where(lead_near, row, far) // 2
    v_rows = pl.ds(vpiece * VPIECE, VPIECE)

    def v_lead_each(act):
        def one(j, carry):
            c = lax.rem(j + col, COLS)

            @pl.when(jnp.logical_or(c == row, (c < row) == lead_near))
            def _():
                slot = jnp.where(jnp.logical_or(c != row, lead_near), 0, 1)
                act(vline.at[lead_src], vbuf.at[slot, v_rows], vf_send.at[j], v_recv.at[slot],
                    row, c, row, col)

            return carry

        lax.fori_loop(0, COLS, one, 0)

        @pl.when(jnp.logical_not(lead_near))
        def _():
            for k in range(2):
                act(vline.at[lead_src, pl.ds(k * ZPIECE, ZPIECE)], vd, vd_send.at[k], vd_recv,
                    row, 2 * vpiece + k, row, col)

    def v_other_each(act, before):
        for j, step in enumerate(((0, 0),) + LINE):
            src = line_row(step)
            tile = 2 * src + parity

            @pl.when(jnp.logical_and(tile <= far, src != lead_src))
            def _():
                before(src)

            @pl.when(tile < row)
            def _():
                act(vline.at[src], vbuf.at[1, v_rows], vo_send.at[j, 0], v_recv.at[1],
                    row, tile, row, col)

            @pl.when(tile < far)
            def _():
                act(vline.at[src], vbuf.at[1, v_rows], vo_send.at[j, 1], v_recv.at[1],
                    row, tile + row + 1, row, col)

    arrived(vline.at[lead_src], vl_recv.at[lead_src])
    v_lead_each(put)
    v_other_each(put, lambda src: arrived(vline.at[src], vl_recv.at[src]))

    @pl.when(jnp.logical_and(vtile > far, lead_src != row))
    def _():
        arrived(vline.at[row], vl_recv.at[row])

    split_part(2)
    split_part(3)

    @pl.when(diag)
    def _():
        rr = lax.broadcasted_iota(jnp.int32, (256, 256), 0)
        cc = lax.broadcasted_iota(jnp.int32, (256, 256), 1)
        for p in range(6):
            at = slice(p * 256, p * 256 + 256)
            block = abuf[at, at]
            lower = jnp.where(rr > cc, block, 0.0)
            upper = jnp.where(rr < cc, block, 0.0)
            onto = jnp.where(rr == cc, block, 0.0)
            far_onto = jnp.where(rr == cc, jnp.broadcast_to(lowd[:, at], (256, 256)), 0.0)
            for s, full in ((0, lower + lower.T + onto), (1, upper + upper.T + far_onto)):
                high, low = halves(full)
                sym[s, 0, p] = high
                sym[s, 1, p] = low

    def cat_v(s):
        for p in range(6):
            at = slice(p * 256, p * 256 + 256)
            high, low = halves(vbuf[s, at, :])
            vcat[s, at, 0:128] = high
            vcat[s, at, 128:256] = low

    def cat_vt(s):
        for p in range(6):
            at = slice(p * 256, p * 256 + 256)
            high, low = halves(vbuf[s, at, :].T)
            vtc[s, 0:128, at] = high
            vtc[s, 128:256, at] = low

    def times(high, low, v):
        full = dot(high, v)
        return full[:, 0:128] + full[:, 128:256] + dot(low, v[:, 0:128])

    def times_t(vt, high, low):
        full = dot(vt, high)
        return full[0:128] + full[128:256] + dot(vt[0:128], low)

    def z_put_range(s, first, count, act=None):
        act = act or put

        def one(j, carry):
            c = first + lax.rem(j + col, count)
            act(z.at[s, pl.ds(c * ZPIECE, ZPIECE)], parts.at[s, col], r_send.at[s, c],
                r_recv.at[s], row, c, row, col)
            return carry

        lax.fori_loop(0, count, one, 0)

    def gram(s):
        high, low = halves(z[s])
        full = dot(vtc[s], high)
        return full[0:128] + full[128:256] + dot(vtc[s, 0:128, :], low)

    def g_start():
        def one(j, carry):
            c = lax.rem(j + col, COLS)
            put(gpart.at[pl.ds(pl.multiple_of(c * 8, 8), 8)], g1.at[col], g_send.at[0, c],
                g_recv.at[0], row, c, row, col)
            return carry

        lax.fori_loop(0, COLS, one, 0)

    arrived(vbuf.at[0], v_recv.at[0])
    cat_vt(0)

    @pl.when(plain)
    def _():
        def panel(k, carry):
            at = pl.ds(pl.multiple_of(k * 768, 768), 768)
            part = times_t(vtc[0], ahi[:, at], alo[:, at])
            z[1, at, :] = part.T
            z_put_range(1, k * 8, 8)
            return carry

        lax.fori_loop(0, 2, panel, 0)

    arrived(vbuf.at[1], v_recv.at[1])
    cat_v(1)

    @pl.when(plain)
    def _():
        def panel(k, carry):
            rows = pl.ds(pl.multiple_of(k * 384, 384), 384)
            z[0, rows, :] = times(ahi[rows, :], alo[rows, :], vcat[1])
            return carry

        lax.fori_loop(0, 4, panel, 0)
        y = gram(0)
        gpart[...] = y + y.T
        g_start()
        z_put_range(0, 0, 16)

    @pl.when(diag)
    def _():
        cat_v(0)
        cat_vt(1)
        for p in range(6):
            lo, hi = p * 256, p * 256 + 256
            at = slice(lo, hi)
            z0 = times(sym[0, 0, p], sym[0, 1, p], vcat[0, at, :])
            z1 = times(sym[1, 0, p], sym[1, 1, p], vcat[1, at, :])
            if p > 0:
                z0 += times(ahi[at, 0:lo], alo[at, 0:lo], vcat[0, 0:lo, :])
                z1 += times_t(vtc[1, :, 0:lo], ahi[0:lo, at], alo[0:lo, at]).T
            if p < 5:
                z1 += times(ahi[at, hi:], alo[at, hi:], vcat[1, hi:, :])
                z0 += times_t(vtc[0, :, hi:], ahi[hi:, at], alo[hi:, at]).T
            z[0, at, :] = z0
            z[1, at, :] = z1
        z_put_range(1, 0, 16)
        gpart[...] = gram(0) + gram(1)
        g_start()
        z_put_range(0, 0, 16)

    arrived(g1, g_recv.at[0])
    g1s[...] = jnp.sum(g1[...], axis=0)

    def g_line(j, carry):
        r = lax.rem(j + row, ROWS)
        put(g1s, g2.at[row], g_send.at[1, r], g_recv.at[1], r, col, row, col)
        return carry

    lax.fori_loop(0, ROWS, g_line, 0)

    arrived(parts.at[1], r_recv.at[1])
    for step in LINE:
        to = line_row(step)

        @pl.when(to < row)
        def _():
            lsend[to] = parts[1, to] + parts[1, to + row + 1]

    def l_copy(src, to, k):
        return pltpu.make_async_remote_copy(
            src_ref=src, dst_ref=lpart.at[row, k], send_sem=l_send.at[to, k],
            recv_sem=l_recv.at[row], device_id=(to, col), device_id_type=MESH,
        )

    def l_each(act):
        for step in LINE:
            to = line_row(step)

            @pl.when(to < row)
            def _():
                act(l_copy(lsend.at[to], to, 0))

            @pl.when(to > row)
            def _():
                act(l_copy(parts.at[1, to + row + 1], to, 0))
                act(l_copy(parts.at[1, GRID - to + row], to, 1))

    l_each(lambda copy: copy.start())

    arrived(g2, g_recv.at[1])
    g2s[...] = jnp.sum(g2[...], axis=0)

    def g_row(j, carry):
        c = lax.rem(j + col, COLS)
        put(g2s, gf.at[pl.ds(pl.multiple_of(col * 8, 8), 8)], g_send.at[2, c], g_recv.at[2],
            row, c, row, col)
        return carry

    lax.fori_loop(0, COLS, g_row, 0)

    arrived(parts.at[0], r_recv.at[0])
    zsum[0] = parts[1, 2 * row + 1]
    zsum[1] = parts[1, row]

    def add_lead(c, carry):
        zsum[jnp.where(c <= row, 0, 1)] += parts[0, c]
        return carry

    lax.fori_loop(0, COLS, add_lead, 0)
    for step in LINE:
        src = line_row(step)

        @pl.when(src < row)
        def _():
            arrived(lpart.at[src], l_recv.at[src])
            zsum[0] += lpart[src, 0]
            zsum[1] += lpart[src, 1]

        @pl.when(src > row)
        def _():
            arrived(lpart.at[src, 0], l_recv.at[src])
            zsum[0] += lpart[src, 0]

    def zf_args(j, half):
        tile = row if half == 0 else GRID - 1 - row
        return member(tile, lax.rem(j + col, 16))

    def zf_put(j, carry):
        for half in range(2):
            to_row, to_col, slot = zf_args(j, half)
            put(zsum.at[half], zf.at[slot, pl.ds(col * ZPIECE, ZPIECE)], z_send.at[half, j],
                z_recv.at[slot], to_row, to_col, row, col)
        return carry

    lax.fori_loop(0, 16, zf_put, 0)

    arrived(gf, g_recv.at[2])
    fac_value = fac[...]
    middle = dot_exact(dot_exact(fac_value, gf[...], ((0,), (0,))), fac_value)

    arrived(vd, vd_recv)
    v_far = vd[...]
    w_far = dot_exact(zsum[1], fac_value) - 0.5 * dot_exact(v_far, middle)
    sums = dot_exact(jnp.ones((8, 128), F32), v_far * w_far, ((1,), (1,)))
    dmine[...] = jnp.concatenate([sums, jnp.zeros((8, 32), F32)], axis=1)

    def d_put(j, carry):
        c = lax.rem(j + col, COLS)
        put(dmine, d_out.at[col], d_send.at[c], d_recv, row, c, row, col)
        return carry

    lax.fori_loop(0, COLS, d_put, 0)

    both = jnp.concatenate([fac_value, -0.5 * middle], axis=0)
    both_high, both_low = halves(both)
    both_t = both.T
    both_t_high, both_t_low = halves(both_t)

    def w_plain(s, out):
        def panel(k, carry):
            rows = pl.ds(pl.multiple_of(k * 256, 256), 256)
            v_high, v_low = halves(vbuf[s, rows, :])
            z_high, z_low = halves(zf[s, rows, :])
            high = jnp.concatenate([z_high, v_high], axis=1)
            low = jnp.concatenate([z_low, v_low], axis=1)
            w = dot(high, both_high) + dot(high, both_low) + dot(low, both_high)
            w_high, w_low = halves(w)
            out[rows, :] = jnp.concatenate([v_high, w_high, v_low, w_low], axis=1)
            return carry

        lax.fori_loop(0, 6, panel, 0)

    def w_turned(s, out):
        def panel(k, carry):
            rows = pl.ds(pl.multiple_of(k * 256, 256), 256)
            v_high, v_low = halves(vbuf[s, rows, :].T)
            z_high, z_low = halves(zf[s, rows, :].T)
            high = jnp.concatenate([z_high, v_high], axis=0)
            low = jnp.concatenate([z_low, v_low], axis=0)
            w = dot(both_t_high, high) + dot(both_t_low, high) + dot(both_t_high, low)
            w_high, w_low = halves(w)
            out[:, rows] = jnp.concatenate([w_high, v_high, w_low, v_low], axis=0)
            return carry

        lax.fori_loop(0, 6, panel, 0)

    arrived(zf.at[1], z_recv.at[1])
    w_turned(1, xrt)
    pltpu.make_async_copy(xrt, xrt_out, o_sem.at[0]).start()
    arrived(zf.at[0], z_recv.at[0])
    w_plain(0, xl)
    pltpu.make_async_copy(xl, xl_out, o_sem.at[1]).start()

    @pl.when(diag)
    def _():
        w_plain(1, xl1)
        w_turned(0, xrt0)
        pltpu.make_async_copy(xl1, xl1_out, o_sem.at[2]).start()
        pltpu.make_async_copy(xrt0, xrt0_out, o_sem.at[3]).start()

    arrived(d_out, d_recv)

    v_line_each(lambda copy: copy.wait_send())
    v_lead_each(sent)
    v_other_each(sent, lambda src: None)
    z_put_range(0, 0, 16, sent)
    z_put_range(1, 0, 16, sent)
    l_each(lambda copy: copy.wait_send())

    def all_sent(j, carry):
        for half in range(2):
            to_row, to_col, slot = zf_args(j, half)
            sent(zsum.at[half], zsum.at[half], z_send.at[half, j], None,
                 to_row, to_col, row, col)
        sent(g1s, g1s, g_send.at[0, j], None, row, j, row, col)
        sent(g2s, g2s, g_send.at[2, j], None, row, j, row, col)
        sent(dmine, dmine, d_send.at[j], None, row, j, row, col)
        return carry

    lax.fori_loop(0, 16, all_sent, 0)

    def line_sent(j, carry):
        sent(g1s, g1s, g_send.at[1, j], None, j, col, row, col)
        return carry

    lax.fori_loop(0, ROWS, line_sent, 0)

    arrived(xrt, o_sem.at[0])
    arrived(xl, o_sem.at[1])

    @pl.when(diag)
    def _():
        arrived(xl1, o_sem.at[2])
        arrived(xrt0, o_sem.at[3])


def update(mat, xl, xrt, d, fard, xl1_hbm, xrt0_hbm, out, far_out, xl1, xrt0, sem):
    step = pl.program_id(0)
    diag = lax.axis_index("row") == lax.axis_index("col")

    @pl.when(jnp.logical_and(diag, step == 0))
    def _():
        first = pltpu.make_async_copy(xl1_hbm, xl1, sem.at[0])
        second = pltpu.make_async_copy(xrt0_hbm, xrt0, sem.at[1])
        first.start()
        second.start()
        first.wait()
        second.wait()

    @pl.when(step == 0)
    def _():
        lane = lax.broadcasted_iota(jnp.int32, (128, TILE), 1)
        start = jnp.zeros((128, TILE), jnp.int32)
        for k in range(1, 16):
            start += jnp.where(lane >= k * ZPIECE, ZPIECE, 0)
        pick = jnp.where(lane - start == lax.broadcasted_iota(jnp.int32, (128, TILE), 0), 1.0, 0.0)
        spread = dot_exact(d[:, 0, :], pick)
        piece = lax.broadcasted_iota(jnp.int32, (16, TILE), 0) * ZPIECE
        whole = jnp.sum(jnp.where(piece == start[0:16], spread, 0.0), axis=0, keepdims=True)
        far_out[...] = fard[...] - 2.0 * whole

    def change(left, right):
        high, low = left[:, 0:256], left[:, 256:512]
        return dot(high, right[0:256]) + dot(high, right[256:512]) + dot(low, right[0:256])

    rows = pl.ds(pl.multiple_of(step * 256, 256), 256)

    @pl.when(jnp.logical_not(diag))
    def _():
        out[...] = mat[...] - change(xl[rows, :], xrt[...])

    @pl.when(diag)
    def _():
        lead = change(xl[rows, :], xrt0[...])
        far = change(xl1[rows, :], xrt[...])
        at_row = lax.broadcasted_iota(jnp.int32, (256, TILE), 0) + step * 256
        at_col = lax.broadcasted_iota(jnp.int32, (256, TILE), 1)
        out[...] = mat[...] - jnp.where(at_row >= at_col, lead, far)


def body(matrix, far_diag, vectors, factors):
    any_spec = pl.BlockSpec(memory_space=pl.ANY)
    vmem_spec = pl.BlockSpec(memory_space=pltpu.VMEM)
    dma = pltpu.SemaphoreType.DMA
    xl_shape = jax.ShapeDtypeStruct((TILE, 512), BF16)
    xrt_shape = jax.ShapeDtypeStruct((512, TILE), BF16)
    xl, xrt, xl1, xrt0, d = pl.pallas_call(
        exchange,
        name="exchange",
        out_shape=(xl_shape, xrt_shape, xl_shape, xrt_shape,
                   jax.ShapeDtypeStruct((16, 8, 128), F32)),
        in_specs=[any_spec, vmem_spec, vmem_spec, vmem_spec],
        out_specs=(any_spec, any_spec, any_spec, any_spec, vmem_spec),
        scratch_shapes=[
            pltpu.VMEM((TILE, TILE), F32),
            pltpu.VMEM((TILE, TILE), BF16),
            pltpu.VMEM((TILE, TILE), BF16),
            pltpu.VMEM((2, 2, 6, 256, 256), BF16),
            pltpu.VMEM((ROWS, VPIECE, NB), F32),
            pltpu.VMEM((2, TILE, NB), F32),
            pltpu.VMEM((2, TILE, 2 * NB), BF16),
            pltpu.VMEM((2, 2 * NB, TILE), BF16),
            pltpu.VMEM((2, TILE, NB), F32),
            pltpu.VMEM((2, COLS, ZPIECE, NB), F32),
            pltpu.VMEM((ROWS, 2, ZPIECE, NB), F32),
            pltpu.VMEM((ROWS, ZPIECE, NB), F32),
            pltpu.VMEM((2, ZPIECE, NB), F32),
            pltpu.VMEM((2, TILE, NB), F32),
            pltpu.VMEM((ZPIECE, NB), F32),
            pltpu.VMEM((NB, NB), F32),
            pltpu.VMEM((16, 8, NB), F32),
            pltpu.VMEM((8, NB), F32),
            pltpu.VMEM((8, 8, NB), F32),
            pltpu.VMEM((8, NB), F32),
            pltpu.VMEM((NB, NB), F32),
            pltpu.VMEM((8, NB), F32),
            pltpu.VMEM((TILE, 512), BF16),
            pltpu.VMEM((512, TILE), BF16),
            pltpu.VMEM((TILE, 512), BF16),
            pltpu.VMEM((512, TILE), BF16),
            dma((4,)),
            dma((8,)),
            dma((8,)),
            dma((16,)),
            dma((8, 2)),
            dma((2,)),
            dma((2,)),
            dma,
            dma((2, 16)),
            dma((2,)),
            dma((8, 2)),
            dma((8,)),
            dma((3, 16)),
            dma((3,)),
            dma((2, 16)),
            dma((2,)),
            dma((16,)),
            dma,
            dma((4,)),
        ],
        compiler_params=pltpu.CompilerParams(
            collective_id=0, has_side_effects=True, vmem_limit_bytes=56 * 2**20
        ),
    )(matrix, far_diag, vectors, factors)
    whole = lambda *shape: pl.BlockSpec(shape, lambda i: (0,) * len(shape))
    updated, far_updated = pl.pallas_call(
        update,
        name="update",
        grid=(6,),
        out_shape=(jax.ShapeDtypeStruct((TILE, TILE), F32), jax.ShapeDtypeStruct((1, TILE), F32)),
        in_specs=[
            pl.BlockSpec((256, TILE), lambda i: (i, 0)),
            whole(TILE, 512),
            whole(512, TILE),
            whole(16, 8, 128),
            whole(1, TILE),
            any_spec,
            any_spec,
        ],
        out_specs=(pl.BlockSpec((256, TILE), lambda i: (i, 0)), whole(1, TILE)),
        scratch_shapes=[
            pltpu.VMEM((TILE, 512), BF16),
            pltpu.VMEM((512, TILE), BF16),
            dma((2,)),
        ],
        compiler_params=pltpu.CompilerParams(vmem_limit_bytes=48 * 2**20),
    )(matrix, xl, xrt, d, far_diag, xl1, xrt0)
    return updated, far_updated


def solution(mesh):
    in_specs = (P("row", "col"), P("row", None), P(("row", "col"), None), P())
    out_specs = (P("row", "col"), P("row", None))
    return jax.shard_map(body, mesh=mesh, in_specs=in_specs, out_specs=out_specs, check_vma=False)
```

```python
import functools

import jax
import jax.numpy as jnp
from jax import lax
from jax.experimental import pallas as pl
from jax.experimental.pallas import tpu as pltpu
from jax.sharding import PartitionSpec as P

TILE = 1536
NB = 128
GRID = 16
HALF = 8
ROWS = 8
LINE = ((0, 1), (1, 0), (3, 0), (1, 1), (3, 1), (2, 0), (2, 1))
COLS = 16
VPIECE = 192
ZPIECE = 96
WIDTH = 256
PEERS = ((0, 0), (0, 1), (1, 0), (0, 3), (3, 0), (1, 1), (3, 3), (1, 3), (3, 1), (0, 2), (2, 0),
         (2, 1), (1, 2), (2, 3), (3, 2), (2, 2))
MESH = pl.DeviceIdType.MESH
F32 = jnp.float32
BF16 = jnp.bfloat16


def dot(left, right):
    return lax.dot_general(left, right, (((1,), (0,)), ((), ())), preferred_element_type=F32)


def dot_exact(left, right, dims=((1,), (0,))):
    return lax.dot_general(
        left, right, (dims, ((), ())), preferred_element_type=F32, precision=lax.Precision.HIGHEST
    )


def halves(value):
    high = value.astype(BF16)
    low = (value - high.astype(F32)).astype(BF16)
    return high, low


def choose(j, values):
    out = jnp.int32(values[0])
    for k, value in enumerate(values):
        if k > 0 and value != values[0]:
            out = jnp.where(j == k, value, out)
    return out


def put(src, dst, send_sem, recv_sem, to_row, to_col, row, col):
    here = jnp.logical_and(to_row == row, to_col == col)

    @pl.when(here)
    def _():
        pltpu.make_async_copy(src, dst, recv_sem).start()

    @pl.when(jnp.logical_not(here))
    def _():
        pltpu.make_async_remote_copy(
            src_ref=src, dst_ref=dst, send_sem=send_sem, recv_sem=recv_sem,
            device_id=(to_row, to_col), device_id_type=MESH,
        ).start()


def sent(src, dst, send_sem, recv_sem, to_row, to_col, row, col):
    here = jnp.logical_and(to_row == row, to_col == col)

    @pl.when(jnp.logical_not(here))
    def _():
        pltpu.make_async_remote_copy(
            src_ref=src, dst_ref=src, send_sem=send_sem, recv_sem=send_sem,
            device_id=(to_row, to_col), device_id_type=MESH,
        ).wait_send()


def arrived(ref, sem):
    pltpu.make_async_copy(ref, ref, sem).wait()


def exchange(
    mat, lowd, vec, fac, x_out, d_out,
    abuf, bhi, blo, vline, vbuf, vcat, vtc, z, zt, parts, lpart, lsend, zsum, zf, vd,
    gpart, g1, g1s, g2, g2s, gf, dmine, xbuf,
    a_sem, vl_send, vl_recv, vf_send, vo_send, v_recv, vd_send, vd_recv, r_send, r_recv,
    l_send, l_recv, g_send, g_recv, z_send, z_recv, d_send, d_recv, o_sem,
):
    row = lax.axis_index("row")
    col = lax.axis_index("col")
    diag = row == col
    plain = row != col
    other = jnp.where(col < row, col, jnp.where(diag, GRID - 1 - row, col - row - 1))
    far = GRID - 1 - row
    x, core = row // 2, lax.rem(row, 2)

    sign = 1 - 2 * core

    def peer(j):
        z = lax.rem(col // 4 + sign * choose(j, [p[0] for p in PEERS]) + 4, 4)
        y = lax.rem(lax.rem(col, 4) + sign * choose(j, [p[1] for p in PEERS]) + 4, 4)
        return z * 4 + y

    def line_row(step):
        return lax.rem(x + step[0], 4) * 2 + lax.rem(core + step[1], 2)

    def part_copy(k):
        return pltpu.make_async_copy(
            mat.at[pl.ds(k * 384, 384)], abuf.at[pl.ds(k * 384, 384)], a_sem.at[k]
        )

    for k in range(4):
        part_copy(k).start()

    bar = pltpu.get_barrier_semaphore()

    def greet(j, carry):
        pl.semaphore_signal(
            bar, inc=1, device_id=(row, lax.rem(col + j, COLS)), device_id_type=MESH
        )
        return carry

    lax.fori_loop(1, COLS, greet, 0)
    for step in LINE:
        pl.semaphore_signal(bar, inc=1, device_id=(line_row(step), col), device_id_type=MESH)

    own = pltpu.make_async_copy(vec, vline.at[row], vl_recv.at[row])
    own.start()

    def split_part(k):
        part_copy(k).wait()

        @pl.when(plain)
        def _():
            def split(s, carry):
                rows = pl.ds(pl.multiple_of(k * 384 + s * 32, 32), 32)
                high, low = halves(abuf[rows, :])
                bhi[0, rows, :] = high
                blo[0, rows, :] = low
                return carry

            lax.fori_loop(0, 12, split, 0)

    split_part(0)
    split_part(1)
    pl.semaphore_wait(bar, COLS - 1 + ROWS - 1)

    vtile = 2 * row + col // 8
    vpiece = lax.rem(col, 8)
    parity = col // 8
    vlead_row = jnp.where(vtile < HALF, vtile, GRID - 1 - vtile)

    def v_line(j, to_row):
        return pltpu.make_async_remote_copy(
            src_ref=vec, dst_ref=vline.at[row], send_sem=vl_send.at[j],
            recv_sem=vl_recv.at[row], device_id=(to_row, col), device_id_type=MESH,
        )

    def v_line_lead(act):
        @pl.when(vlead_row != row)
        def _():
            act(v_line(7, vlead_row))

    def v_line_each(act):
        for j, step in enumerate(LINE):
            to_row = line_row(step)

            @pl.when(jnp.logical_and(to_row != vlead_row, to_row <= GRID - 1 - vtile))
            def _():
                act(v_line(j, to_row))

    v_line_lead(lambda copy: copy.start())

    lead_near = lax.rem(row, 2) == parity
    lead_src = jnp.where(lead_near, row, far) // 2
    v_rows = pl.ds(vpiece * VPIECE, VPIECE)

    def v_lead_each(act):
        def one(j, carry):
            c = peer(j)

            @pl.when(jnp.logical_or(c == row, (c < row) == lead_near))
            def _():
                slot = jnp.where(jnp.logical_and(c == row, lead_near), 1, 0)
                act(vline.at[lead_src], vbuf.at[slot, v_rows], vf_send.at[j], v_recv.at[slot],
                    row, c, row, col)

            return carry

        lax.fori_loop(0, COLS, one, 0)

        @pl.when(jnp.logical_not(lead_near))
        def _():
            for k in range(2):
                act(vline.at[lead_src, pl.ds(k * ZPIECE, ZPIECE)], vd, vd_send.at[k], vd_recv,
                    row, 2 * vpiece + k, row, col)

    def v_other_each(act, before):
        for j, step in enumerate(((0, 0),) + LINE):
            src = line_row(step)
            tile = 2 * src + parity

            @pl.when(jnp.logical_and(tile <= far, src != lead_src))
            def _():
                before(src)

            @pl.when(tile < row)
            def _():
                act(vline.at[src], vbuf.at[1, v_rows], vo_send.at[j, 0], v_recv.at[1],
                    row, tile, row, col)

            @pl.when(tile < far)
            def _():
                act(vline.at[src], vbuf.at[1, v_rows], vo_send.at[j, 1], v_recv.at[1],
                    row, tile + row + 1, row, col)

    arrived(vline.at[lead_src], vl_recv.at[lead_src])
    v_lead_each(put)
    v_line_each(lambda copy: copy.start())
    v_other_each(put, lambda src: arrived(vline.at[src], vl_recv.at[src]))

    @pl.when(jnp.logical_and(vtile > far, lead_src != row))
    def _():
        arrived(vline.at[row], vl_recv.at[row])

    split_part(2)
    split_part(3)

    @pl.when(diag)
    def _():
        def keep(s, rows, cols, value):
            high, low = halves(value)
            bhi[s, rows, cols] = high
            blo[s, rows, cols] = low

        def block_at(n, carry):
            p, q = n // 6, lax.rem(n, 6)
            rows = pl.ds(pl.multiple_of(p * 256, 256), 256)
            cols = pl.ds(pl.multiple_of(q * 256, 256), 256)

            @pl.when(p != q)
            def _():
                s = jnp.where(p > q, 0, 1)
                block = abuf[rows, cols]
                keep(s, rows, cols, block)
                keep(s, cols, rows, block.T)

            @pl.when(p == q)
            def _():
                block = abuf[rows, cols]
                rr = lax.broadcasted_iota(jnp.int32, (256, 256), 0)
                cc = lax.broadcasted_iota(jnp.int32, (256, 256), 1)
                lower = jnp.where(rr > cc, block, 0.0)
                upper = jnp.where(rr < cc, block, 0.0)
                onto = jnp.where(rr == cc, block, 0.0)
                far_onto = jnp.where(rr == cc, jnp.broadcast_to(lowd[:, cols], (256, 256)), 0.0)
                keep(0, rows, cols, lower + lower.T + onto)
                keep(1, rows, cols, upper + upper.T + far_onto)

            return carry

        lax.fori_loop(0, 36, block_at, 0)

    def cat_v(s):
        for p in range(6):
            at = slice(p * 256, p * 256 + 256)
            high, low = halves(vbuf[s, at, :])
            vcat[s, at, 0:128] = high
            vcat[s, at, 128:256] = low

    def cat_vt(s):
        for p in range(6):
            at = slice(p * 256, p * 256 + 256)
            high, low = halves(vbuf[s, at, :].T)
            vtc[s, 0:128, at] = high
            vtc[s, 128:256, at] = low

    def times(high, low, v):
        full = dot(high, v)
        return full[:, 0:128] + full[:, 128:256] + dot(low, v[:, 0:128])

    def times_t(vt, high, low):
        full = dot(vt, high)
        return full[0:128] + full[128:256] + dot(vt[0:128], low)

    def z_put(s, act=put):
        def one(j, carry):
            c = peer(j)
            act(z.at[s, pl.ds(c * ZPIECE, ZPIECE)], parts.at[s, col], r_send.at[s, c],
                r_recv.at[s], row, c, row, col)
            return carry

        lax.fori_loop(0, COLS, one, 0)

    def g_start():
        def one(j, carry):
            c = lax.rem(j + col, COLS)
            put(gpart.at[pl.ds(pl.multiple_of(c * 8, 8), 8)], g1.at[col], g_send.at[0, c],
                g_recv.at[0], row, c, row, col)
            return carry

        lax.fori_loop(0, COLS, one, 0)

    second = jnp.where(diag, 1, 0)
    arrived(vbuf.at[0], v_recv.at[0])
    cat_vt(0)

    def turned_panel(k, carry):
        at = pl.ds(pl.multiple_of(k * 768, 768), 768)
        part = times_t(vtc[0], bhi[second, :, at], blo[second, :, at])
        zt[:, at] = part
        z[1, at, :] = part.T
        return carry

    lax.fori_loop(0, 2, turned_panel, 0)
    z_put(1)

    arrived(vbuf.at[1], v_recv.at[1])
    cat_v(1)

    @pl.when(plain)
    def _():
        high, low = halves(zt[...])
        y = times(high, low, vcat[1])
        gpart[...] = y + y.T
        g_start()

    def panel(k, carry):
        rows = pl.ds(pl.multiple_of(k * 384, 384), 384)
        z[0, rows, :] = times(bhi[0, rows, :], blo[0, rows, :], vcat[1])
        return carry

    lax.fori_loop(0, 4, panel, 0)
    z_put(0)

    @pl.when(diag)
    def _():
        cat_v(0)
        cat_vt(1)
        high, low = halves(zt[...])
        y = times(high, low, vcat[0])
        high, low = halves(z[0])
        full = dot(vtc[1], high)
        gpart[...] = y + full[0:128] + full[128:256] + dot(vtc[1, 0:128, :], low)
        g_start()

    arrived(parts.at[1], r_recv.at[1])
    for step in LINE:
        to = line_row(step)

        @pl.when(to < row)
        def _():
            lsend[to] = parts[1, to] + parts[1, to + row + 1]

    def l_copy(src, to, k):
        return pltpu.make_async_remote_copy(
            src_ref=src, dst_ref=lpart.at[row, k], send_sem=l_send.at[to, k],
            recv_sem=l_recv.at[row], device_id=(to, col), device_id_type=MESH,
        )

    def l_each(act):
        for step in LINE:
            to = line_row(step)

            @pl.when(to < row)
            def _():
                act(l_copy(lsend.at[to], to, 0))

            @pl.when(to > row)
            def _():
                act(l_copy(parts.at[1, to + row + 1], to, 0))
                act(l_copy(parts.at[1, GRID - to + row], to, 1))

    l_each(lambda copy: copy.start())

    arrived(g1, g_recv.at[0])
    g1s[...] = jnp.sum(g1[...], axis=0)

    def g_line(j, carry):
        r = lax.rem(j + row, ROWS)
        put(g1s, g2.at[row], g_send.at[1, r], g_recv.at[1], r, col, row, col)
        return carry

    lax.fori_loop(0, ROWS, g_line, 0)

    arrived(parts.at[0], r_recv.at[0])
    zsum[0] = parts[1, 2 * row + 1]
    zsum[1] = parts[1, row]

    def add_lead(c, carry):
        zsum[jnp.where(c <= row, 0, 1)] += parts[0, c]
        return carry

    lax.fori_loop(0, COLS, add_lead, 0)
    for step in LINE:
        src = line_row(step)

        @pl.when(src < row)
        def _():
            arrived(lpart.at[src], l_recv.at[src])
            zsum[0] += lpart[src, 0]
            zsum[1] += lpart[src, 1]

        @pl.when(src > row)
        def _():
            arrived(lpart.at[src, 0], l_recv.at[src])
            zsum[0] += lpart[src, 0]

    arrived(g2, g_recv.at[1])
    g2s[...] = jnp.sum(g2[...], axis=0)

    def g_row(j, carry):
        c = lax.rem(j + col, COLS)
        put(g2s, gf.at[pl.ds(pl.multiple_of(col * 8, 8), 8)], g_send.at[2, c], g_recv.at[2],
            row, c, row, col)
        return carry

    lax.fori_loop(0, COLS, g_row, 0)

    def zf_each(act):
        def one(j, carry):
            c = peer(j)
            half = jnp.where(c <= row, 0, 1)
            slot = jnp.where(c == row, 1, 0)
            act(zsum.at[half], zf.at[slot, pl.ds(col * ZPIECE, ZPIECE)], z_send.at[0, j],
                z_recv.at[slot], row, c, row, col)
            to = lax.rem(row + sign * j + 2 * ROWS, ROWS)
            first = j < ROWS
            half = jnp.where(jnp.logical_or(first, to > row), 0, 1)
            slot = jnp.where(jnp.logical_or(first, to != row), 1, 0)
            to_col = jnp.where(
                first, to + row + 1, jnp.where(to >= row, row, GRID - row + to))
            act(zsum.at[half], zf.at[slot, pl.ds(col * ZPIECE, ZPIECE)], z_send.at[1, j],
                z_recv.at[slot], to, to_col, row, col)
            return carry

        lax.fori_loop(0, COLS, one, 0)

    zf_each(put)

    arrived(gf, g_recv.at[2])
    fac_value = fac[...]
    middle = dot_exact(dot_exact(fac_value, gf[...], ((0,), (0,))), fac_value)

    arrived(vd, vd_recv)
    v_far = vd[...]
    w_far = dot_exact(zsum[1], fac_value) - 0.5 * dot_exact(v_far, middle)
    sums = dot_exact(jnp.ones((8, 128), F32), v_far * w_far, ((1,), (1,)))
    dmine[...] = jnp.concatenate([sums, jnp.zeros((8, 32), F32)], axis=1)

    def d_put(j, carry):
        c = lax.rem(j + col, COLS)
        put(dmine, d_out.at[col], d_send.at[c], d_recv, row, c, row, col)
        return carry

    lax.fori_loop(0, COLS, d_put, 0)

    both = jnp.concatenate([fac_value, -0.5 * middle], axis=0)
    both_high, both_low = halves(both)

    def w_into(s):
        def panel(k, carry):
            rows = pl.ds(pl.multiple_of(k * 256, 256), 256)
            v_high, v_low = halves(vbuf[s, rows, :])
            z_high, z_low = halves(zf[s, rows, :])
            high = jnp.concatenate([z_high, v_high], axis=1)
            low = jnp.concatenate([z_low, v_low], axis=1)
            w = dot(high, both_high) + dot(high, both_low) + dot(low, both_high)
            w_high, w_low = halves(w)
            xbuf[s, rows, :] = jnp.concatenate([v_high, w_high, v_low, w_low], axis=1)
            return carry

        lax.fori_loop(0, 6, panel, 0)
        pltpu.make_async_copy(xbuf.at[s], x_out.at[s], o_sem.at[s]).start()

    for s in (1, 0):
        arrived(zf.at[s], z_recv.at[s])
        w_into(s)

    arrived(d_out, d_recv)

    v_line_lead(lambda copy: copy.wait_send())
    v_line_each(lambda copy: copy.wait_send())
    v_lead_each(sent)
    v_other_each(sent, lambda src: None)
    z_put(0, sent)
    z_put(1, sent)
    l_each(lambda copy: copy.wait_send())

    zf_each(sent)

    def all_sent(j, carry):
        sent(g1s, g1s, g_send.at[0, j], None, row, j, row, col)
        sent(g2s, g2s, g_send.at[2, j], None, row, j, row, col)
        sent(dmine, dmine, d_send.at[j], None, row, j, row, col)
        return carry

    lax.fori_loop(0, 16, all_sent, 0)

    def line_sent(j, carry):
        sent(g1s, g1s, g_send.at[1, j], None, j, col, row, col)
        return carry

    lax.fori_loop(0, ROWS, line_sent, 0)

    arrived(xbuf.at[0], o_sem.at[0])
    arrived(xbuf.at[1], o_sem.at[1])


def update(mat, x_hbm, d, fard, out, far_out, abuf, x, sem, in_sem, out_sem):
    diag = lax.axis_index("row") == lax.axis_index("col")
    x_copy = pltpu.make_async_copy(x_hbm, x, sem)
    x_copy.start()

    def columns(k):
        return pl.ds(pl.multiple_of(k * WIDTH, WIDTH), WIDTH)

    def load(k):
        return pltpu.make_async_copy(mat.at[:, columns(k)], abuf.at[:, columns(k)], in_sem.at[k])

    def store(k):
        return pltpu.make_async_copy(abuf.at[:, columns(k)], out.at[:, columns(k)], out_sem.at[k])

    def each(act):
        def one(k, carry):
            act(k)
            return carry

        lax.fori_loop(0, TILE // WIDTH, one, 0)

    each(lambda k: load(k).start())

    lane = lax.broadcasted_iota(jnp.int32, (128, TILE), 1)
    start = jnp.zeros((128, TILE), jnp.int32)
    for k in range(1, 16):
        start += jnp.where(lane >= k * ZPIECE, ZPIECE, 0)
    pick = jnp.where(lane - start == lax.broadcasted_iota(jnp.int32, (128, TILE), 0), 1.0, 0.0)
    spread = dot_exact(d[:, 0, :], pick)
    piece = lax.broadcasted_iota(jnp.int32, (16, TILE), 0) * ZPIECE
    whole = jnp.sum(jnp.where(piece == start[0:16], spread, 0.0), axis=0, keepdims=True)
    far_out[...] = fard[...] - 2.0 * whole
    x_copy.wait()

    def dot_nt(left, right):
        return lax.dot_general(
            left, right, (((1,), (1,)), ((), ())), preferred_element_type=F32
        )

    def change(s, t, cols, rows=slice(None)):
        v_high, w_high = x[t, cols, 0:128], x[t, cols, 128:256]
        v_low, w_low = x[t, cols, 256:384], x[t, cols, 384:512]
        high = jnp.concatenate([w_high, v_high], axis=1)
        low = jnp.concatenate([w_low, v_low], axis=1)
        left_high, left_low = x[s, rows, 0:256], x[s, rows, 256:512]
        return dot_nt(left_high, high) + dot_nt(left_high, low) + dot_nt(left_low, high)

    @pl.when(jnp.logical_not(diag))
    def _():
        def step(k):
            cols = columns(k)
            load(k).wait()
            abuf[:, cols] -= change(0, 1, cols)
            store(k).start()

        each(step)

    @pl.when(diag)
    def _():
        below = lax.broadcasted_iota(jnp.int32, (WIDTH, WIDTH), 0) >= lax.broadcasted_iota(
            jnp.int32, (WIDTH, WIDTH), 1)
        for k in range(TILE // WIDTH):
            lo, hi = k * WIDTH, k * WIDTH + WIDTH
            cols = slice(lo, hi)
            load(k).wait()
            near = change(1, 1, cols, slice(lo, TILE))
            far = change(0, 0, cols, slice(0, hi))
            if k > 0:
                abuf[0:lo, cols] -= far[0:lo]
            abuf[lo:hi, cols] -= jnp.where(below, near[0:WIDTH], far[lo:hi])
            if hi < TILE:
                abuf[hi:, cols] -= near[WIDTH:]
            store(k).start()

    each(lambda k: store(k).wait())


def body(matrix, far_diag, vectors, factors):
    any_spec = pl.BlockSpec(memory_space=pl.ANY)
    vmem_spec = pl.BlockSpec(memory_space=pltpu.VMEM)
    dma = pltpu.SemaphoreType.DMA
    x, d = pl.pallas_call(
        exchange,
        name="exchange",
        out_shape=(jax.ShapeDtypeStruct((2, TILE, 512), BF16),
                   jax.ShapeDtypeStruct((16, 8, 128), F32)),
        in_specs=[any_spec, vmem_spec, vmem_spec, vmem_spec],
        out_specs=(any_spec, vmem_spec),
        scratch_shapes=[
            pltpu.VMEM((TILE, TILE), F32),
            pltpu.VMEM((2, TILE, TILE), BF16),
            pltpu.VMEM((2, TILE, TILE), BF16),
            pltpu.VMEM((ROWS, VPIECE, NB), F32),
            pltpu.VMEM((2, TILE, NB), F32),
            pltpu.VMEM((2, TILE, 2 * NB), BF16),
            pltpu.VMEM((2, 2 * NB, TILE), BF16),
            pltpu.VMEM((2, TILE, NB), F32),
            pltpu.VMEM((NB, TILE), F32),
            pltpu.VMEM((2, COLS, ZPIECE, NB), F32),
            pltpu.VMEM((ROWS, 2, ZPIECE, NB), F32),
            pltpu.VMEM((ROWS, ZPIECE, NB), F32),
            pltpu.VMEM((2, ZPIECE, NB), F32),
            pltpu.VMEM((2, TILE, NB), F32),
            pltpu.VMEM((ZPIECE, NB), F32),
            pltpu.VMEM((NB, NB), F32),
            pltpu.VMEM((16, 8, NB), F32),
            pltpu.VMEM((8, NB), F32),
            pltpu.VMEM((8, 8, NB), F32),
            pltpu.VMEM((8, NB), F32),
            pltpu.VMEM((NB, NB), F32),
            pltpu.VMEM((8, NB), F32),
            pltpu.VMEM((2, TILE, 512), BF16),
            dma((4,)),
            dma((8,)),
            dma((8,)),
            dma((16,)),
            dma((8, 2)),
            dma((2,)),
            dma((2,)),
            dma,
            dma((2, 16)),
            dma((2,)),
            dma((8, 2)),
            dma((8,)),
            dma((3, 16)),
            dma((3,)),
            dma((2, 16)),
            dma((2,)),
            dma((16,)),
            dma,
            dma((2,)),
        ],
        compiler_params=pltpu.CompilerParams(
            collective_id=0, has_side_effects=True, vmem_limit_bytes=56 * 2**20
        ),
    )(matrix, far_diag, vectors, factors)
    updated, far_updated = pl.pallas_call(
        update,
        name="update",
        out_shape=(jax.ShapeDtypeStruct((TILE, TILE), F32), jax.ShapeDtypeStruct((1, TILE), F32)),
        in_specs=[any_spec, any_spec, vmem_spec, vmem_spec],
        out_specs=(any_spec, vmem_spec),
        scratch_shapes=[
            pltpu.VMEM((TILE, TILE), F32),
            pltpu.VMEM((2, TILE, 512), BF16),
            dma,
            dma((TILE // WIDTH,)),
            dma((TILE // WIDTH,)),
        ],
        compiler_params=pltpu.CompilerParams(vmem_limit_bytes=60 * 2**20),
    )(matrix, x, d, far_diag)
    return updated, far_updated


def solution(mesh):
    in_specs = (P("row", "col"), P("row", None), P(("row", "col"), None), P())
    out_specs = (P("row", "col"), P("row", None))
    return jax.shard_map(body, mesh=mesh, in_specs=in_specs, out_specs=out_specs, check_vma=False)
```

```python
import functools

import jax
import jax.numpy as jnp
from jax import lax
from jax.experimental import pallas as pl
from jax.experimental.pallas import tpu as pltpu
from jax.sharding import PartitionSpec as P

TILE = 1536
NB = 128
GRID = 16
HALF = 8
ROWS = 8
LINE = ((0, 1), (1, 0), (3, 0), (1, 1), (3, 1), (2, 0), (2, 1))
COLS = 16
VPIECE = 192
ZPIECE = 96
WIDTH = 256
PEERS = ((0, 0), (0, 1), (1, 0), (0, 3), (3, 0), (1, 1), (3, 3), (1, 3), (3, 1), (0, 2), (2, 0),
         (2, 1), (1, 2), (2, 3), (3, 2), (2, 2))
MESH = pl.DeviceIdType.MESH
F32 = jnp.float32
BF16 = jnp.bfloat16


def dot(left, right):
    return lax.dot_general(left, right, (((1,), (0,)), ((), ())), preferred_element_type=F32)


def dot_exact(left, right, dims=((1,), (0,))):
    return lax.dot_general(
        left, right, (dims, ((), ())), preferred_element_type=F32, precision=lax.Precision.HIGHEST
    )


def halves(value):
    high = value.astype(BF16)
    low = (value - high.astype(F32)).astype(BF16)
    return high, low


def choose(j, values):
    out = jnp.int32(values[0])
    for k, value in enumerate(values):
        if k > 0 and value != values[0]:
            out = jnp.where(j == k, value, out)
    return out


def put(src, dst, send_sem, recv_sem, to_row, to_col, row, col):
    here = jnp.logical_and(to_row == row, to_col == col)

    @pl.when(here)
    def _():
        pltpu.make_async_copy(src, dst, recv_sem).start()

    @pl.when(jnp.logical_not(here))
    def _():
        pltpu.make_async_remote_copy(
            src_ref=src, dst_ref=dst, send_sem=send_sem, recv_sem=recv_sem,
            device_id=(to_row, to_col), device_id_type=MESH,
        ).start()


def sent(src, dst, send_sem, recv_sem, to_row, to_col, row, col):
    here = jnp.logical_and(to_row == row, to_col == col)

    @pl.when(jnp.logical_not(here))
    def _():
        pltpu.make_async_remote_copy(
            src_ref=src, dst_ref=src, send_sem=send_sem, recv_sem=send_sem,
            device_id=(to_row, to_col), device_id_type=MESH,
        ).wait_send()


def arrived(ref, sem):
    pltpu.make_async_copy(ref, ref, sem).wait()


def exchange(
    mat, lowd, vec, fac, x_out, d_out,
    abuf, bhi, blo, vline, vz, vbuf, vcat, vtc, z, zt, parts, lpart, lsend, zsum, zf, vd,
    gpart, g1, g1s, g2, g2s, gf, dmine, xbuf,
    a_sem, vl_send, vl_recv, vz_send, vz_recv, vf_send, vo_send, v_recv, vd_send, vd_recv, r_send, r_recv,
    l_send, l_recv, g_send, g_recv, z_send, z_recv, d_send, d_recv, o_sem,
):
    row = lax.axis_index("row")
    col = lax.axis_index("col")
    diag = row == col
    plain = row != col
    other = jnp.where(col < row, col, jnp.where(diag, GRID - 1 - row, col - row - 1))
    far = GRID - 1 - row
    x, core = row // 2, lax.rem(row, 2)

    sign = 1 - 2 * core

    def peer(j):
        z = lax.rem(col // 4 + sign * choose(j, [p[0] for p in PEERS]) + 4, 4)
        y = lax.rem(lax.rem(col, 4) + sign * choose(j, [p[1] for p in PEERS]) + 4, 4)
        return z * 4 + y

    def line_row(step):
        return lax.rem(x + step[0], 4) * 2 + lax.rem(core + step[1], 2)

    def part_copy(k):
        return pltpu.make_async_copy(
            mat.at[pl.ds(k * 384, 384)], abuf.at[pl.ds(k * 384, 384)], a_sem.at[k]
        )

    for k in range(4):
        part_copy(k).start()

    bar = pltpu.get_barrier_semaphore()

    def greet(j, carry):
        pl.semaphore_signal(
            bar, inc=1, device_id=(row, lax.rem(col + j, COLS)), device_id_type=MESH
        )
        return carry

    lax.fori_loop(1, COLS, greet, 0)
    for step in LINE:
        pl.semaphore_signal(bar, inc=1, device_id=(line_row(step), col), device_id_type=MESH)

    own = pltpu.make_async_copy(vec, vline.at[row], vl_recv.at[row])
    own.start()

    def split_part(k):
        part_copy(k).wait()

        @pl.when(plain)
        def _():
            def split(s, carry):
                rows = pl.ds(pl.multiple_of(k * 384 + s * 32, 32), 32)
                high, low = halves(abuf[rows, :])
                bhi[0, rows, :] = high
                blo[0, rows, :] = low
                return carry

            lax.fori_loop(0, 12, split, 0)

    split_part(0)
    split_part(1)
    pl.semaphore_wait(bar, COLS - 1 + ROWS - 1)

    vtile = 2 * row + col // 8
    vpiece = lax.rem(col, 8)
    parity = col // 8
    vlead_row = jnp.where(vtile < HALF, vtile, GRID - 1 - vtile)

    def v_line(j, to_row):
        return pltpu.make_async_remote_copy(
            src_ref=vec, dst_ref=vline.at[row], send_sem=vl_send.at[j],
            recv_sem=vl_recv.at[row], device_id=(to_row, col), device_id_type=MESH,
        )

    def v_line_lead(act):
        @pl.when(vlead_row != row)
        def _():
            act(v_line(7, vlead_row))

    def v_line_each(act):
        for j, step in enumerate(LINE):
            to_row = line_row(step)

            @pl.when(jnp.logical_and(to_row != vlead_row, to_row <= GRID - 1 - vtile))
            def _():
                act(v_line(j, to_row))

    v_line_lead(lambda copy: copy.start())

    lead_near = lax.rem(row, 2) == parity
    lead_src = jnp.where(lead_near, row, far) // 2
    v_rows = pl.ds(vpiece * VPIECE, VPIECE)

    z_at, y_at = col // 4, lax.rem(col, 4)
    z_row = row // 4

    def v_lead_each(act):
        for j, dz in enumerate((0, 1, 3, 2)):
            to_z = lax.rem(z_at + sign * dz + 4, 4)

            @pl.when(jnp.logical_or(to_z == z_row, (to_z < z_row) == lead_near))
            def _():
                act(vline.at[lead_src], vz.at[z_at], vz_send.at[j], vz_recv.at[z_at],
                    row, to_z * 4 + y_at, row, col)

        @pl.when(jnp.logical_not(lead_near))
        def _():
            for k in range(2):
                act(vline.at[lead_src, pl.ds(k * ZPIECE, ZPIECE)], vd, vd_send.at[k], vd_recv,
                    row, 2 * vpiece + k, row, col)

    def v_hand_each(act, before):
        for j, dz in enumerate((0, 1, 3, 2)):
            src = lax.rem(z_at - sign * dz + 4, 4)
            near = lax.rem(row, 2) == src // 2

            @pl.when(jnp.logical_or(z_at == z_row, (z_at < z_row) == near))
            def _():
                before(src)

                for i, dy in enumerate((0, 1, 3, 2)):
                    c = z_at * 4 + lax.rem(y_at + sign * dy + 4, 4)

                    @pl.when(jnp.logical_or(c == row, (c < row) == near))
                    def _():
                        slot = jnp.where(jnp.logical_and(c == row, near), 1, 0)
                        rows = pl.ds((lax.rem(src, 2) * 4 + y_at) * VPIECE, VPIECE)
                        act(vz.at[src], vbuf.at[slot, rows], vf_send.at[j, i], v_recv.at[slot],
                            row, c, row, col)

    def v_other_each(act, before, first_j=0, last_j=ROWS):
        for j, step in list(enumerate(((0, 0),) + LINE))[first_j:last_j]:
            src = line_row(step)
            tile = 2 * src + parity

            @pl.when(jnp.logical_and(tile <= far, src != lead_src))
            def _():
                before(src)

            @pl.when(tile < row)
            def _():
                act(vec if j == 0 else vline.at[src], vbuf.at[1, v_rows], vo_send.at[j, 0], v_recv.at[1],
                    row, tile, row, col)

            @pl.when(tile < far)
            def _():
                act(vec if j == 0 else vline.at[src], vbuf.at[1, v_rows], vo_send.at[j, 1], v_recv.at[1],
                    row, tile + row + 1, row, col)

    v_other_each(put, lambda src: arrived(vline.at[src], vl_recv.at[src]), 0, 1)
    arrived(vline.at[lead_src], vl_recv.at[lead_src])
    v_lead_each(put)
    v_line_each(lambda copy: copy.start())
    v_hand_each(put, lambda src: arrived(vz.at[src], vz_recv.at[src]))
    v_other_each(put, lambda src: arrived(vline.at[src], vl_recv.at[src]), 1)

    @pl.when(jnp.logical_and(vtile > far, lead_src != row))
    def _():
        arrived(vline.at[row], vl_recv.at[row])

    split_part(2)
    split_part(3)

    @pl.when(diag)
    def _():
        def keep(s, rows, cols, value):
            high, low = halves(value)
            bhi[s, rows, cols] = high
            blo[s, rows, cols] = low

        def block_at(n, carry):
            p, q = n // 6, lax.rem(n, 6)
            rows = pl.ds(pl.multiple_of(p * 256, 256), 256)
            cols = pl.ds(pl.multiple_of(q * 256, 256), 256)

            @pl.when(p != q)
            def _():
                s = jnp.where(p > q, 0, 1)
                block = abuf[rows, cols]
                keep(s, rows, cols, block)
                keep(s, cols, rows, block.T)

            @pl.when(p == q)
            def _():
                block = abuf[rows, cols]
                rr = lax.broadcasted_iota(jnp.int32, (256, 256), 0)
                cc = lax.broadcasted_iota(jnp.int32, (256, 256), 1)
                lower = jnp.where(rr > cc, block, 0.0)
                upper = jnp.where(rr < cc, block, 0.0)
                onto = jnp.where(rr == cc, block, 0.0)
                far_onto = jnp.where(rr == cc, jnp.broadcast_to(lowd[:, cols], (256, 256)), 0.0)
                keep(0, rows, cols, lower + lower.T + onto)
                keep(1, rows, cols, upper + upper.T + far_onto)

            return carry

        lax.fori_loop(0, 36, block_at, 0)

    def cat_v(s):
        for p in range(6):
            at = slice(p * 256, p * 256 + 256)
            high, low = halves(vbuf[s, at, :])
            vcat[s, at, 0:128] = high
            vcat[s, at, 128:256] = low

    def cat_vt(s):
        for p in range(6):
            at = slice(p * 256, p * 256 + 256)
            high, low = halves(vbuf[s, at, :].T)
            vtc[s, 0:128, at] = high
            vtc[s, 128:256, at] = low

    def times(high, low, v):
        full = dot(high, v)
        return full[:, 0:128] + full[:, 128:256] + dot(low, v[:, 0:128])

    def times_t(vt, high, low):
        full = dot(vt, high)
        return full[0:128] + full[128:256] + dot(vt[0:128], low)

    def z_put(s, act=put, half=None):
        def one(j, carry):
            c = peer(j)

            @pl.when(True if half is None else c // 8 == half)
            def _():
                act(z.at[s, pl.ds(c * ZPIECE, ZPIECE)], parts.at[s, col], r_send.at[s, c],
                    r_recv.at[s], row, c, row, col)

            return carry

        lax.fori_loop(0, COLS, one, 0)

    def g_start():
        def one(j, carry):
            c = lax.rem(j + col, COLS)
            put(gpart.at[pl.ds(pl.multiple_of(c * 8, 8), 8)], g1.at[col], g_send.at[0, c],
                g_recv.at[0], row, c, row, col)
            return carry

        lax.fori_loop(0, COLS, one, 0)

    second = jnp.where(diag, 1, 0)
    arrived(vbuf.at[0], v_recv.at[0])
    cat_vt(0)

    def turned_panel(n, carry):
        k = lax.rem(n + z_at // 2, 2)
        at = pl.ds(pl.multiple_of(k * 768, 768), 768)
        part = times_t(vtc[0], bhi[second, :, at], blo[second, :, at])
        zt[:, at] = part
        z[1, at, :] = part.T
        z_put(1, half=k)
        return carry

    lax.fori_loop(0, 2, turned_panel, 0)

    arrived(vbuf.at[1], v_recv.at[1])
    cat_v(1)

    @pl.when(plain)
    def _():
        high, low = halves(zt[...])
        y = times(high, low, vcat[1])
        gpart[...] = y + y.T
        g_start()

    def panel(n, carry):
        k = lax.rem(n + z_at // 2, 2)
        rows = pl.ds(pl.multiple_of(k * 768, 768), 768)
        z[0, rows, :] = times(bhi[0, rows, :], blo[0, rows, :], vcat[1])
        z_put(0, half=k)
        return carry

    lax.fori_loop(0, 2, panel, 0)

    @pl.when(diag)
    def _():
        cat_v(0)
        cat_vt(1)
        high, low = halves(zt[...])
        y = times(high, low, vcat[0])
        high, low = halves(z[0])
        full = dot(vtc[1], high)
        gpart[...] = y + full[0:128] + full[128:256] + dot(vtc[1, 0:128, :], low)
        g_start()

    arrived(parts.at[1], r_recv.at[1])
    for step in LINE:
        to = line_row(step)

        @pl.when(to < row)
        def _():
            lsend[to] = parts[1, to] + parts[1, to + row + 1]

    def l_copy(src, to, k):
        return pltpu.make_async_remote_copy(
            src_ref=src, dst_ref=lpart.at[row, k], send_sem=l_send.at[to, k],
            recv_sem=l_recv.at[row], device_id=(to, col), device_id_type=MESH,
        )

    def l_each(act):
        for step in LINE:
            to = line_row(step)

            @pl.when(to < row)
            def _():
                act(l_copy(lsend.at[to], to, 0))

            @pl.when(to > row)
            def _():
                act(l_copy(parts.at[1, to + row + 1], to, 0))
                act(l_copy(parts.at[1, GRID - to + row], to, 1))

    l_each(lambda copy: copy.start())

    arrived(g1, g_recv.at[0])
    g1s[...] = jnp.sum(g1[...], axis=0)

    def g_line(j, carry):
        r = lax.rem(j + row, ROWS)
        put(g1s, g2.at[row], g_send.at[1, r], g_recv.at[1], r, col, row, col)
        return carry

    lax.fori_loop(0, ROWS, g_line, 0)

    arrived(parts.at[0], r_recv.at[0])
    zsum[0] = parts[1, 2 * row + 1]
    zsum[1] = parts[1, row]

    def add_lead(c, carry):
        zsum[jnp.where(c <= row, 0, 1)] += parts[0, c]
        return carry

    lax.fori_loop(0, COLS, add_lead, 0)
    for step in LINE:
        src = line_row(step)

        @pl.when(src < row)
        def _():
            arrived(lpart.at[src], l_recv.at[src])
            zsum[0] += lpart[src, 0]
            zsum[1] += lpart[src, 1]

        @pl.when(src > row)
        def _():
            arrived(lpart.at[src, 0], l_recv.at[src])
            zsum[0] += lpart[src, 0]

    def zf_each(first_j, last_j, act):
        def one(j, carry):
            c = peer(j)
            half = jnp.where(c <= row, 0, 1)
            slot = jnp.where(c == row, 1, 0)
            act(zsum.at[half], zf.at[slot, pl.ds(col * ZPIECE, ZPIECE)], z_send.at[0, j],
                z_recv.at[slot, z_at], row, c, row, col)
            to = lax.rem(row + sign * j + 2 * ROWS, ROWS)
            first = j < ROWS
            half = jnp.where(jnp.logical_or(first, to > row), 0, 1)
            slot = jnp.where(jnp.logical_or(first, to != row), 1, 0)
            to_col = jnp.where(
                first, to + row + 1, jnp.where(to >= row, row, GRID - row + to))
            act(zsum.at[half], zf.at[slot, pl.ds(col * ZPIECE, ZPIECE)], z_send.at[1, j],
                z_recv.at[slot, z_at], to, to_col, row, col)
            return carry

        lax.fori_loop(first_j, last_j, one, 0)

    zf_each(0, 6, put)
    arrived(g2, g_recv.at[1])
    g2s[...] = jnp.sum(g2[...], axis=0)

    def g_row(j, carry):
        c = lax.rem(j + col, COLS)
        put(g2s, gf.at[pl.ds(pl.multiple_of(col * 8, 8), 8)], g_send.at[2, c], g_recv.at[2],
            row, c, row, col)
        return carry

    lax.fori_loop(0, COLS, g_row, 0)
    zf_each(6, COLS, put)

    arrived(gf, g_recv.at[2])
    fac_value = fac[...]
    middle = dot_exact(dot_exact(fac_value, gf[...], ((0,), (0,))), fac_value)

    arrived(vd, vd_recv)
    v_far = vd[...]
    w_far = dot_exact(zsum[1], fac_value) - 0.5 * dot_exact(v_far, middle)
    sums = dot_exact(jnp.ones((8, 128), F32), v_far * w_far, ((1,), (1,)))
    dmine[...] = jnp.concatenate([sums, jnp.zeros((8, 32), F32)], axis=1)

    def d_put(j, carry):
        c = lax.rem(j + col, COLS)
        put(dmine, d_out.at[col], d_send.at[c], d_recv, row, c, row, col)
        return carry

    lax.fori_loop(0, COLS, d_put, 0)

    both = jnp.concatenate([fac_value, -0.5 * middle], axis=0)
    both_high, both_low = halves(both)

    def w_into(step):
        k = lax.rem(z_at + step, 4)

        def one(s, carry):
            rows = pl.ds(pl.multiple_of(k * 384, 384), 384)
            arrived(zf.at[s, rows], z_recv.at[s, k])
            v_high, v_low = halves(vbuf[s, rows, :])
            z_high, z_low = halves(zf[s, rows, :])
            high = jnp.concatenate([z_high, v_high], axis=1)
            low = jnp.concatenate([z_low, v_low], axis=1)
            w = dot(high, both_high) + dot(high, both_low) + dot(low, both_high)
            w_high, w_low = halves(w)
            xbuf[s, rows, :] = jnp.concatenate([v_high, w_high, v_low, w_low], axis=1)
            pltpu.make_async_copy(xbuf.at[s, rows], x_out.at[s, rows], o_sem.at[s, k]).start()
            return carry

        lax.fori_loop(0, 2, one, 0)

    for step in (0, 1, 3, 2):
        w_into(step)

    arrived(d_out, d_recv)

    v_line_lead(lambda copy: copy.wait_send())
    v_line_each(lambda copy: copy.wait_send())
    v_lead_each(sent)
    v_hand_each(sent, lambda src: None)
    v_other_each(sent, lambda src: None)
    z_put(0, sent)
    z_put(1, sent)
    l_each(lambda copy: copy.wait_send())

    zf_each(0, COLS, sent)

    def all_sent(j, carry):
        sent(g1s, g1s, g_send.at[0, j], None, row, j, row, col)
        sent(g2s, g2s, g_send.at[2, j], None, row, j, row, col)
        sent(dmine, dmine, d_send.at[j], None, row, j, row, col)
        return carry

    lax.fori_loop(0, 16, all_sent, 0)

    def line_sent(j, carry):
        sent(g1s, g1s, g_send.at[1, j], None, j, col, row, col)
        return carry

    lax.fori_loop(0, ROWS, line_sent, 0)

    for s in range(2):
        for k in range(4):
            arrived(xbuf.at[s, pl.ds(k * 384, 384)], o_sem.at[s, k])


def update(mat, x_hbm, d, fard, out, far_out, abuf, x, sem, in_sem, out_sem):
    diag = lax.axis_index("row") == lax.axis_index("col")
    x_copy = pltpu.make_async_copy(x_hbm, x, sem)
    x_copy.start()

    def columns(k):
        return pl.ds(pl.multiple_of(k * WIDTH, WIDTH), WIDTH)

    def load(k):
        return pltpu.make_async_copy(mat.at[:, columns(k)], abuf.at[:, columns(k)], in_sem.at[k])

    def store(k):
        return pltpu.make_async_copy(abuf.at[:, columns(k)], out.at[:, columns(k)], out_sem.at[k])

    def each(act):
        def one(k, carry):
            act(k)
            return carry

        lax.fori_loop(0, TILE // WIDTH, one, 0)

    each(lambda k: load(k).start())

    lane = lax.broadcasted_iota(jnp.int32, (128, TILE), 1)
    start = jnp.zeros((128, TILE), jnp.int32)
    for k in range(1, 16):
        start += jnp.where(lane >= k * ZPIECE, ZPIECE, 0)
    pick = jnp.where(lane - start == lax.broadcasted_iota(jnp.int32, (128, TILE), 0), 1.0, 0.0)
    spread = dot_exact(d[:, 0, :], pick)
    piece = lax.broadcasted_iota(jnp.int32, (16, TILE), 0) * ZPIECE
    whole = jnp.sum(jnp.where(piece == start[0:16], spread, 0.0), axis=0, keepdims=True)
    far_out[...] = fard[...] - 2.0 * whole
    x_copy.wait()

    def dot_nt(left, right):
        return lax.dot_general(
            left, right, (((1,), (1,)), ((), ())), preferred_element_type=F32
        )

    def change(s, t, cols, rows=slice(None)):
        v_high, w_high = x[t, cols, 0:128], x[t, cols, 128:256]
        v_low, w_low = x[t, cols, 256:384], x[t, cols, 384:512]
        high = jnp.concatenate([w_high, v_high], axis=1)
        low = jnp.concatenate([w_low, v_low], axis=1)
        left_high, left_low = x[s, rows, 0:256], x[s, rows, 256:512]
        return dot_nt(left_high, high) + dot_nt(left_high, low) + dot_nt(left_low, high)

    @pl.when(jnp.logical_not(diag))
    def _():
        def step(k):
            cols = columns(k)
            load(k).wait()
            abuf[:, cols] -= change(0, 1, cols)
            store(k).start()

        each(step)

    @pl.when(diag)
    def _():
        below = lax.broadcasted_iota(jnp.int32, (WIDTH, WIDTH), 0) >= lax.broadcasted_iota(
            jnp.int32, (WIDTH, WIDTH), 1)
        for k in range(TILE // WIDTH):
            lo, hi = k * WIDTH, k * WIDTH + WIDTH
            cols = slice(lo, hi)
            load(k).wait()
            near = change(1, 1, cols, slice(lo, TILE))
            far = change(0, 0, cols, slice(0, hi))
            if k > 0:
                abuf[0:lo, cols] -= far[0:lo]
            abuf[lo:hi, cols] -= jnp.where(below, near[0:WIDTH], far[lo:hi])
            if hi < TILE:
                abuf[hi:, cols] -= near[WIDTH:]
            store(k).start()

    each(lambda k: store(k).wait())


def body(matrix, far_diag, vectors, factors):
    any_spec = pl.BlockSpec(memory_space=pl.ANY)
    vmem_spec = pl.BlockSpec(memory_space=pltpu.VMEM)
    dma = pltpu.SemaphoreType.DMA
    x, d = pl.pallas_call(
        exchange,
        name="exchange",
        out_shape=(jax.ShapeDtypeStruct((2, TILE, 512), BF16),
                   jax.ShapeDtypeStruct((16, 8, 128), F32)),
        in_specs=[any_spec, vmem_spec, vmem_spec, vmem_spec],
        out_specs=(any_spec, vmem_spec),
        scratch_shapes=[
            pltpu.VMEM((TILE, TILE), F32),
            pltpu.VMEM((2, TILE, TILE), BF16),
            pltpu.VMEM((2, TILE, TILE), BF16),
            pltpu.VMEM((ROWS, VPIECE, NB), F32),
            pltpu.VMEM((4, VPIECE, NB), F32),
            pltpu.VMEM((2, TILE, NB), F32),
            pltpu.VMEM((2, TILE, 2 * NB), BF16),
            pltpu.VMEM((2, 2 * NB, TILE), BF16),
            pltpu.VMEM((2, TILE, NB), F32),
            pltpu.VMEM((NB, TILE), F32),
            pltpu.VMEM((2, COLS, ZPIECE, NB), F32),
            pltpu.VMEM((ROWS, 2, ZPIECE, NB), F32),
            pltpu.VMEM((ROWS, ZPIECE, NB), F32),
            pltpu.VMEM((2, ZPIECE, NB), F32),
            pltpu.VMEM((2, TILE, NB), F32),
            pltpu.VMEM((ZPIECE, NB), F32),
            pltpu.VMEM((NB, NB), F32),
            pltpu.VMEM((16, 8, NB), F32),
            pltpu.VMEM((8, NB), F32),
            pltpu.VMEM((8, 8, NB), F32),
            pltpu.VMEM((8, NB), F32),
            pltpu.VMEM((NB, NB), F32),
            pltpu.VMEM((8, NB), F32),
            pltpu.VMEM((2, TILE, 512), BF16),
            dma((4,)),
            dma((8,)),
            dma((8,)),
            dma((4,)),
            dma((4,)),
            dma((4, 4)),
            dma((8, 2)),
            dma((2,)),
            dma((2,)),
            dma,
            dma((2, 16)),
            dma((2,)),
            dma((8, 2)),
            dma((8,)),
            dma((3, 16)),
            dma((3,)),
            dma((2, 16)),
            dma((2, 4)),
            dma((16,)),
            dma,
            dma((2, 4)),
        ],
        compiler_params=pltpu.CompilerParams(
            collective_id=0, has_side_effects=True, vmem_limit_bytes=56 * 2**20
        ),
    )(matrix, far_diag, vectors, factors)
    updated, far_updated = pl.pallas_call(
        update,
        name="update",
        out_shape=(jax.ShapeDtypeStruct((TILE, TILE), F32), jax.ShapeDtypeStruct((1, TILE), F32)),
        in_specs=[any_spec, any_spec, vmem_spec, vmem_spec],
        out_specs=(any_spec, vmem_spec),
        scratch_shapes=[
            pltpu.VMEM((TILE, TILE), F32),
            pltpu.VMEM((2, TILE, 512), BF16),
            dma,
            dma((TILE // WIDTH,)),
            dma((TILE // WIDTH,)),
        ],
        compiler_params=pltpu.CompilerParams(vmem_limit_bytes=60 * 2**20),
    )(matrix, x, d, far_diag)
    return updated, far_updated


def solution(mesh):
    in_specs = (P("row", "col"), P("row", None), P(("row", "col"), None), P())
    out_specs = (P("row", "col"), P("row", None))
    return jax.shard_map(body, mesh=mesh, in_specs=in_specs, out_specs=out_specs, check_vma=False)
```

```python
import functools

import jax
import jax.numpy as jnp
from jax import lax
from jax.experimental import pallas as pl
from jax.experimental.pallas import tpu as pltpu
from jax.sharding import PartitionSpec as P

TILE = 1536
NB = 128
GRID = 16
HALF = 8
ROWS = 8
LINE = ((0, 1), (1, 0), (3, 0), (1, 1), (3, 1), (2, 0), (2, 1))
COLS = 16
VPIECE = 192
ZPIECE = 96
WIDTH = 512
PEERS = ((0, 0), (0, 1), (1, 0), (0, 3), (3, 0), (1, 1), (3, 3), (1, 3), (3, 1), (0, 2), (2, 0),
         (2, 1), (1, 2), (2, 3), (3, 2), (2, 2))
MESH = pl.DeviceIdType.MESH
F32 = jnp.float32
BF16 = jnp.bfloat16


def dot(left, right):
    return lax.dot_general(left, right, (((1,), (0,)), ((), ())), preferred_element_type=F32)


def dot_exact(left, right, dims=((1,), (0,))):
    return lax.dot_general(
        left, right, (dims, ((), ())), preferred_element_type=F32, precision=lax.Precision.HIGHEST
    )


def halves(value):
    high = value.astype(BF16)
    low = (value - high.astype(F32)).astype(BF16)
    return high, low


def choose(j, values):
    out = jnp.int32(values[0])
    for k, value in enumerate(values):
        if k > 0 and value != values[0]:
            out = jnp.where(j == k, value, out)
    return out


def put(src, dst, send_sem, recv_sem, to_row, to_col, row, col):
    here = jnp.logical_and(to_row == row, to_col == col)

    @pl.when(here)
    def _():
        pltpu.make_async_copy(src, dst, recv_sem).start()

    @pl.when(jnp.logical_not(here))
    def _():
        pltpu.make_async_remote_copy(
            src_ref=src, dst_ref=dst, send_sem=send_sem, recv_sem=recv_sem,
            device_id=(to_row, to_col), device_id_type=MESH,
        ).start()


def sent(src, dst, send_sem, recv_sem, to_row, to_col, row, col):
    here = jnp.logical_and(to_row == row, to_col == col)

    @pl.when(jnp.logical_not(here))
    def _():
        pltpu.make_async_remote_copy(
            src_ref=src, dst_ref=src, send_sem=send_sem, recv_sem=send_sem,
            device_id=(to_row, to_col), device_id_type=MESH,
        ).wait_send()


def arrived(ref, sem):
    pltpu.make_async_copy(ref, ref, sem).wait()


def exchange(
    mat, lowd, vec, fac, x_out, d_out,
    abuf, bhi, blo, vline, vz, vbuf, vcat, vtc, z, zt, parts, lpart, lsend, zsum, zf, vd,
    gpart, g1, g1s, g2, g2s, gf, dmine, xbuf,
    a_sem, vl_send, vl_recv, vz_send, vz_recv, vf_send, vo_send, v_recv, vd_send, vd_recv, r_send, r_recv,
    l_send, l_recv, g_send, g_recv, z_send, z_recv, d_send, d_recv, o_sem,
):
    row = lax.axis_index("row")
    col = lax.axis_index("col")
    diag = row == col
    plain = row != col
    other = jnp.where(col < row, col, jnp.where(diag, GRID - 1 - row, col - row - 1))
    far = GRID - 1 - row
    x, core = row // 2, lax.rem(row, 2)

    sign = 1 - 2 * core

    def peer(j):
        z = lax.rem(col // 4 + sign * choose(j, [p[0] for p in PEERS]) + 4, 4)
        y = lax.rem(lax.rem(col, 4) + sign * choose(j, [p[1] for p in PEERS]) + 4, 4)
        return z * 4 + y

    def line_row(step):
        return lax.rem(x + step[0], 4) * 2 + lax.rem(core + step[1], 2)

    def part_copy(k):
        return pltpu.make_async_copy(
            mat.at[pl.ds(k * 384, 384)], abuf.at[pl.ds(k * 384, 384)], a_sem.at[k]
        )

    for k in range(4):
        part_copy(k).start()

    bar = pltpu.get_barrier_semaphore()

    def greet(j, carry):
        pl.semaphore_signal(
            bar, inc=1, device_id=(row, lax.rem(col + j, COLS)), device_id_type=MESH
        )
        return carry

    lax.fori_loop(1, COLS, greet, 0)
    for step in LINE:
        pl.semaphore_signal(bar, inc=1, device_id=(line_row(step), col), device_id_type=MESH)

    own = pltpu.make_async_copy(vec, vline.at[row], vl_recv.at[row])
    own.start()

    def split_part(k):
        part_copy(k).wait()

        @pl.when(plain)
        def _():
            def split(s, carry):
                rows = pl.ds(pl.multiple_of(k * 384 + s * 32, 32), 32)
                high, low = halves(abuf[rows, :])
                bhi[0, rows, :] = high
                blo[0, rows, :] = low
                return carry

            lax.fori_loop(0, 12, split, 0)

    pl.semaphore_wait(bar, COLS - 1 + ROWS - 1)

    vtile = 2 * row + col // 8
    vpiece = lax.rem(col, 8)
    parity = col // 8
    vlead_row = jnp.where(vtile < HALF, vtile, GRID - 1 - vtile)

    def v_line(j, to_row):
        return pltpu.make_async_remote_copy(
            src_ref=vec, dst_ref=vline.at[row], send_sem=vl_send.at[j],
            recv_sem=vl_recv.at[row], device_id=(to_row, col), device_id_type=MESH,
        )

    def v_line_lead(act):
        @pl.when(vlead_row != row)
        def _():
            act(v_line(7, vlead_row))

    def v_line_each(act):
        for j, step in enumerate(LINE):
            to_row = line_row(step)

            @pl.when(jnp.logical_and(to_row != vlead_row, to_row <= GRID - 1 - vtile))
            def _():
                act(v_line(j, to_row))

    v_line_lead(lambda copy: copy.start())

    lead_near = lax.rem(row, 2) == parity
    lead_src = jnp.where(lead_near, row, far) // 2
    v_rows = pl.ds(vpiece * VPIECE, VPIECE)

    z_at, y_at = col // 4, lax.rem(col, 4)
    z_row = row // 4

    def v_lead_each(act):
        for j, dz in enumerate((0, 1, 3, 2)):
            to_z = lax.rem(z_at + sign * dz + 4, 4)

            @pl.when(jnp.logical_or(to_z == z_row, (to_z < z_row) == lead_near))
            def _():
                act(vline.at[lead_src], vz.at[z_at], vz_send.at[j], vz_recv.at[z_at],
                    row, to_z * 4 + y_at, row, col)

        @pl.when(jnp.logical_not(lead_near))
        def _():
            for k in range(2):
                act(vline.at[lead_src, pl.ds(k * ZPIECE, ZPIECE)], vd, vd_send.at[k], vd_recv,
                    row, 2 * vpiece + k, row, col)

    def v_hand_each(act, before):
        for j, dz in enumerate((0, 1, 3, 2)):
            src = lax.rem(z_at - sign * dz + 4, 4)
            near = lax.rem(row, 2) == src // 2

            @pl.when(jnp.logical_or(z_at == z_row, (z_at < z_row) == near))
            def _():
                before(src)

                for i, dy in enumerate((0, 1, 3, 2)):
                    c = z_at * 4 + lax.rem(y_at + sign * dy + 4, 4)

                    @pl.when(jnp.logical_or(c == row, (c < row) == near))
                    def _():
                        slot = jnp.where(jnp.logical_and(c == row, near), 1, 0)
                        rows = pl.ds((lax.rem(src, 2) * 4 + y_at) * VPIECE, VPIECE)
                        act(vz.at[src], vbuf.at[slot, rows], vf_send.at[j, i], v_recv.at[slot],
                            row, c, row, col)

    def v_other_each(act, before):
        def one(j, carry):
            q = lax.rem(j + vpiece, ROWS)
            steps = ((0, 0),) + LINE
            src = line_row((choose(q, [p[0] for p in steps]), choose(q, [p[1] for p in steps])))
            tile = 2 * src + parity

            @pl.when(jnp.logical_and(tile <= far, src != lead_src))
            def _():
                before(src)

            @pl.when(tile < row)
            def _():
                act(vline.at[src], vbuf.at[1, v_rows], vo_send.at[q, 0], v_recv.at[1],
                    row, tile, row, col)

            @pl.when(tile < far)
            def _():
                act(vline.at[src], vbuf.at[1, v_rows], vo_send.at[q, 1], v_recv.at[1],
                    row, tile + row + 1, row, col)

            return carry

        lax.fori_loop(0, ROWS, one, 0)

    split_part(0)
    arrived(vline.at[lead_src], vl_recv.at[lead_src])
    v_lead_each(put)
    v_line_each(lambda copy: copy.start())
    v_hand_each(put, lambda src: arrived(vz.at[src], vz_recv.at[src]))
    v_other_each(put, lambda src: arrived(vline.at[src], vl_recv.at[src]))

    @pl.when(jnp.logical_and(vtile > far, lead_src != row))
    def _():
        arrived(vline.at[row], vl_recv.at[row])

    split_part(1)
    split_part(2)
    split_part(3)

    @pl.when(diag)
    def _():
        def keep(s, rows, cols, value):
            high, low = halves(value)
            bhi[s, rows, cols] = high
            blo[s, rows, cols] = low

        def block_at(n, carry):
            p, q = n // 6, lax.rem(n, 6)
            rows = pl.ds(pl.multiple_of(p * 256, 256), 256)
            cols = pl.ds(pl.multiple_of(q * 256, 256), 256)

            @pl.when(p != q)
            def _():
                s = jnp.where(p > q, 0, 1)
                block = abuf[rows, cols]
                keep(s, rows, cols, block)
                keep(s, cols, rows, block.T)

            @pl.when(p == q)
            def _():
                block = abuf[rows, cols]
                rr = lax.broadcasted_iota(jnp.int32, (256, 256), 0)
                cc = lax.broadcasted_iota(jnp.int32, (256, 256), 1)
                lower = jnp.where(rr > cc, block, 0.0)
                upper = jnp.where(rr < cc, block, 0.0)
                onto = jnp.where(rr == cc, block, 0.0)
                far_onto = jnp.where(rr == cc, jnp.broadcast_to(lowd[:, cols], (256, 256)), 0.0)
                keep(0, rows, cols, lower + lower.T + onto)
                keep(1, rows, cols, upper + upper.T + far_onto)

            return carry

        lax.fori_loop(0, 36, block_at, 0)

    def cat_v(s):
        for p in range(6):
            at = slice(p * 256, p * 256 + 256)
            high, low = halves(vbuf[s, at, :])
            vcat[s, at, 0:128] = high
            vcat[s, at, 128:256] = low

    def cat_vt(s):
        for p in range(6):
            at = slice(p * 256, p * 256 + 256)
            high, low = halves(vbuf[s, at, :].T)
            vtc[s, 0:128, at] = high
            vtc[s, 128:256, at] = low

    def times(high, low, v):
        full = dot(high, v)
        return full[:, 0:128] + full[:, 128:256] + dot(low, v[:, 0:128])

    def times_t(vt, high, low):
        full = dot(vt, high)
        return full[0:128] + full[128:256] + dot(vt[0:128], low)

    def z_put(s, act=put, half=None):
        def one(j, carry):
            c = peer(j)

            @pl.when(True if half is None else c // 8 == half)
            def _():
                act(z.at[s, pl.ds(c * ZPIECE, ZPIECE)], parts.at[s, col], r_send.at[s, c],
                    r_recv.at[s], row, c, row, col)

            return carry

        lax.fori_loop(0, COLS, one, 0)

    def g_start():
        def one(j, carry):
            c = lax.rem(j + col, COLS)
            put(gpart.at[pl.ds(pl.multiple_of(c * 8, 8), 8)], g1.at[col], g_send.at[0, c],
                g_recv.at[0], row, c, row, col)
            return carry

        lax.fori_loop(0, COLS, one, 0)

    second = jnp.where(diag, 1, 0)
    arrived(vbuf.at[0], v_recv.at[0])
    cat_vt(0)

    def turned_panel(n, carry):
        k = lax.rem(n + z_at // 2, 2)
        at = pl.ds(pl.multiple_of(k * 768, 768), 768)
        part = times_t(vtc[0], bhi[second, :, at], blo[second, :, at])
        zt[:, at] = part
        z[1, at, :] = part.T
        z_put(1, half=k)
        return carry

    lax.fori_loop(0, 2, turned_panel, 0)

    arrived(vbuf.at[1], v_recv.at[1])
    cat_v(1)

    @pl.when(plain)
    def _():
        high, low = halves(zt[...])
        y = times(high, low, vcat[1])
        gpart[...] = y + y.T
        g_start()

    def panel(n, carry):
        k = lax.rem(n + z_at // 2, 2)
        rows = pl.ds(pl.multiple_of(k * 768, 768), 768)
        z[0, rows, :] = times(bhi[0, rows, :], blo[0, rows, :], vcat[1])
        z_put(0, half=k)
        return carry

    lax.fori_loop(0, 2, panel, 0)

    @pl.when(diag)
    def _():
        cat_v(0)
        cat_vt(1)
        high, low = halves(zt[...])
        y = times(high, low, vcat[0])
        high, low = halves(z[0])
        full = dot(vtc[1], high)
        gpart[...] = y + full[0:128] + full[128:256] + dot(vtc[1, 0:128, :], low)
        g_start()

    arrived(parts.at[1], r_recv.at[1])
    for step in LINE:
        to = line_row(step)

        @pl.when(to < row)
        def _():
            lsend[to] = parts[1, to] + parts[1, to + row + 1]

    def l_copy(src, to, k):
        return pltpu.make_async_remote_copy(
            src_ref=src, dst_ref=lpart.at[row, k], send_sem=l_send.at[to, k],
            recv_sem=l_recv.at[row], device_id=(to, col), device_id_type=MESH,
        )

    def l_each(act):
        for step in LINE:
            to = line_row(step)

            @pl.when(to < row)
            def _():
                act(l_copy(lsend.at[to], to, 0))

            @pl.when(to > row)
            def _():
                act(l_copy(parts.at[1, to + row + 1], to, 0))
                act(l_copy(parts.at[1, GRID - to + row], to, 1))

    l_each(lambda copy: copy.start())

    arrived(g1, g_recv.at[0])
    g1s[...] = jnp.sum(g1[...], axis=0)

    def g_line(j, carry):
        r = lax.rem(j + row, ROWS)
        put(g1s, g2.at[row], g_send.at[1, r], g_recv.at[1], r, col, row, col)
        return carry

    lax.fori_loop(0, ROWS, g_line, 0)

    arrived(parts.at[0], r_recv.at[0])
    zsum[0] = parts[1, 2 * row + 1]
    zsum[1] = parts[1, row]

    def add_lead(c, carry):
        zsum[jnp.where(c <= row, 0, 1)] += parts[0, c]
        return carry

    lax.fori_loop(0, COLS, add_lead, 0)
    for step in LINE:
        src = line_row(step)

        @pl.when(src < row)
        def _():
            arrived(lpart.at[src], l_recv.at[src])
            zsum[0] += lpart[src, 0]
            zsum[1] += lpart[src, 1]

        @pl.when(src > row)
        def _():
            arrived(lpart.at[src, 0], l_recv.at[src])
            zsum[0] += lpart[src, 0]

    def zf_each(first_j, last_j, act):
        def one(j, carry):
            c = peer(j)
            half = jnp.where(c <= row, 0, 1)
            slot = jnp.where(c == row, 1, 0)
            act(zsum.at[half], zf.at[slot, pl.ds(col * ZPIECE, ZPIECE)], z_send.at[0, j],
                z_recv.at[slot, z_at], row, c, row, col)
            n = lax.rem(j + col, COLS)
            to = lax.rem(row + n, ROWS)
            first = n < ROWS
            half = jnp.where(jnp.logical_or(first, to > row), 0, 1)
            slot = jnp.where(jnp.logical_or(first, to != row), 1, 0)
            to_col = jnp.where(
                first, to + row + 1, jnp.where(to >= row, row, GRID - row + to))
            act(zsum.at[half], zf.at[slot, pl.ds(col * ZPIECE, ZPIECE)], z_send.at[1, j],
                z_recv.at[slot, z_at], to, to_col, row, col)
            return carry

        lax.fori_loop(first_j, last_j, one, 0)

    zf_each(0, 6, put)
    arrived(g2, g_recv.at[1])
    g2s[...] = jnp.sum(g2[...], axis=0)

    def g_row(j, carry):
        c = lax.rem(j + col, COLS)
        put(g2s, gf.at[pl.ds(pl.multiple_of(col * 8, 8), 8)], g_send.at[2, c], g_recv.at[2],
            row, c, row, col)
        return carry

    lax.fori_loop(0, COLS, g_row, 0)
    zf_each(6, COLS, put)

    arrived(gf, g_recv.at[2])
    fac_value = fac[...]
    middle = dot_exact(dot_exact(fac_value, gf[...], ((0,), (0,))), fac_value)

    arrived(vd, vd_recv)
    v_far = vd[...]
    w_far = dot_exact(zsum[1], fac_value) - 0.5 * dot_exact(v_far, middle)
    sums = dot_exact(jnp.ones((8, 128), F32), v_far * w_far, ((1,), (1,)))
    dmine[...] = jnp.concatenate([sums, jnp.zeros((8, 32), F32)], axis=1)

    def d_put(j, carry):
        c = lax.rem(j + col, COLS)
        put(dmine, d_out.at[col], d_send.at[c], d_recv, row, c, row, col)
        return carry

    lax.fori_loop(0, COLS, d_put, 0)

    both = jnp.concatenate([fac_value, -0.5 * middle], axis=0)
    both_high, both_low = halves(both)

    def w_into(step):
        k = lax.rem(z_at + step, 4)

        def one(s, carry):
            rows = pl.ds(pl.multiple_of(k * 384, 384), 384)
            arrived(zf.at[s, rows], z_recv.at[s, k])
            v_high, v_low = halves(vbuf[s, rows, :])
            z_high, z_low = halves(zf[s, rows, :])
            high = jnp.concatenate([z_high, v_high], axis=1)
            low = jnp.concatenate([z_low, v_low], axis=1)
            w = dot(high, both_high) + dot(high, both_low) + dot(low, both_high)
            w_high, w_low = halves(w)
            xbuf[s, rows, :] = jnp.concatenate([v_high, w_high, v_low, w_low], axis=1)
            pltpu.make_async_copy(xbuf.at[s, rows], x_out.at[s, rows], o_sem.at[s, k]).start()
            return carry

        lax.fori_loop(0, 2, one, 0)

    v_line_lead(lambda copy: copy.wait_send())
    v_line_each(lambda copy: copy.wait_send())
    v_lead_each(sent)
    v_hand_each(sent, lambda src: None)
    v_other_each(sent, lambda src: None)
    z_put(0, sent)
    z_put(1, sent)
    l_each(lambda copy: copy.wait_send())

    def row_sent(j, carry):
        sent(g1s, g1s, g_send.at[0, j], None, row, j, row, col)
        sent(g2s, g2s, g_send.at[2, j], None, row, j, row, col)
        return carry

    lax.fori_loop(0, COLS, row_sent, 0)

    def line_sent(j, carry):
        sent(g1s, g1s, g_send.at[1, j], None, j, col, row, col)
        return carry

    lax.fori_loop(0, ROWS, line_sent, 0)

    w_into(0)
    w_into(1)
    w_into(3)
    zf_each(0, COLS, sent)

    def d_sent(j, carry):
        sent(dmine, dmine, d_send.at[j], None, row, j, row, col)
        return carry

    lax.fori_loop(0, COLS, d_sent, 0)
    w_into(2)

    arrived(d_out, d_recv)

    for s in range(2):
        for k in range(4):
            arrived(xbuf.at[s, pl.ds(k * 384, 384)], o_sem.at[s, k])


def update(mat, x_hbm, d, fard, out, far_out, abuf, x, sem, in_sem, out_sem):
    diag = lax.axis_index("row") == lax.axis_index("col")
    x_copy = pltpu.make_async_copy(x_hbm, x, sem)
    x_copy.start()

    def columns(k):
        return pl.ds(pl.multiple_of(k * WIDTH, WIDTH), WIDTH)

    def load(k):
        return pltpu.make_async_copy(mat.at[:, columns(k)], abuf.at[:, columns(k)], in_sem.at[k])

    def store(k):
        return pltpu.make_async_copy(abuf.at[:, columns(k)], out.at[:, columns(k)], out_sem.at[k])

    def each(act):
        def one(k, carry):
            act(k)
            return carry

        lax.fori_loop(0, TILE // WIDTH, one, 0)

    each(lambda k: load(k).start())

    lane = lax.broadcasted_iota(jnp.int32, (128, TILE), 1)
    start = jnp.zeros((128, TILE), jnp.int32)
    for k in range(1, 16):
        start += jnp.where(lane >= k * ZPIECE, ZPIECE, 0)
    pick = jnp.where(lane - start == lax.broadcasted_iota(jnp.int32, (128, TILE), 0), 1.0, 0.0)
    spread = dot_exact(d[:, 0, :], pick)
    piece = lax.broadcasted_iota(jnp.int32, (16, TILE), 0) * ZPIECE
    whole = jnp.sum(jnp.where(piece == start[0:16], spread, 0.0), axis=0, keepdims=True)
    far_out[...] = fard[...] - 2.0 * whole
    x_copy.wait()

    def dot_nt(left, right):
        return lax.dot_general(
            left, right, (((1,), (1,)), ((), ())), preferred_element_type=F32
        )

    def change(s, t, cols, rows=slice(None)):
        v_high, w_high = x[t, cols, 0:128], x[t, cols, 128:256]
        v_low, w_low = x[t, cols, 256:384], x[t, cols, 384:512]
        high = jnp.concatenate([w_high, v_high], axis=1)
        low = jnp.concatenate([w_low, v_low], axis=1)
        left_high, left_low = x[s, rows, 0:256], x[s, rows, 256:512]
        return dot_nt(left_high, high) + dot_nt(left_high, low) + dot_nt(left_low, high)

    @pl.when(jnp.logical_not(diag))
    def _():
        def step(k):
            cols = columns(k)
            load(k).wait()
            abuf[:, cols] -= change(0, 1, cols)
            store(k).start()

        each(step)

    @pl.when(diag)
    def _():
        below = lax.broadcasted_iota(jnp.int32, (WIDTH, WIDTH), 0) >= lax.broadcasted_iota(
            jnp.int32, (WIDTH, WIDTH), 1)
        for k in range(TILE // WIDTH):
            lo, hi = k * WIDTH, k * WIDTH + WIDTH
            cols = slice(lo, hi)
            load(k).wait()
            near = change(1, 1, cols, slice(lo, TILE))
            far = change(0, 0, cols, slice(0, hi))
            if k > 0:
                abuf[0:lo, cols] -= far[0:lo]
            abuf[lo:hi, cols] -= jnp.where(below, near[0:WIDTH], far[lo:hi])
            if hi < TILE:
                abuf[hi:, cols] -= near[WIDTH:]
            store(k).start()

    each(lambda k: store(k).wait())


def body(matrix, far_diag, vectors, factors):
    any_spec = pl.BlockSpec(memory_space=pl.ANY)
    vmem_spec = pl.BlockSpec(memory_space=pltpu.VMEM)
    dma = pltpu.SemaphoreType.DMA
    x, d = pl.pallas_call(
        exchange,
        name="exchange",
        out_shape=(jax.ShapeDtypeStruct((2, TILE, 512), BF16),
                   jax.ShapeDtypeStruct((16, 8, 128), F32)),
        in_specs=[any_spec, vmem_spec, vmem_spec, vmem_spec],
        out_specs=(any_spec, vmem_spec),
        scratch_shapes=[
            pltpu.VMEM((TILE, TILE), F32),
            pltpu.VMEM((2, TILE, TILE), BF16),
            pltpu.VMEM((2, TILE, TILE), BF16),
            pltpu.VMEM((ROWS, VPIECE, NB), F32),
            pltpu.VMEM((4, VPIECE, NB), F32),
            pltpu.VMEM((2, TILE, NB), F32),
            pltpu.VMEM((2, TILE, 2 * NB), BF16),
            pltpu.VMEM((2, 2 * NB, TILE), BF16),
            pltpu.VMEM((2, TILE, NB), F32),
            pltpu.VMEM((NB, TILE), F32),
            pltpu.VMEM((2, COLS, ZPIECE, NB), F32),
            pltpu.VMEM((ROWS, 2, ZPIECE, NB), F32),
            pltpu.VMEM((ROWS, ZPIECE, NB), F32),
            pltpu.VMEM((2, ZPIECE, NB), F32),
            pltpu.VMEM((2, TILE, NB), F32),
            pltpu.VMEM((ZPIECE, NB), F32),
            pltpu.VMEM((NB, NB), F32),
            pltpu.VMEM((16, 8, NB), F32),
            pltpu.VMEM((8, NB), F32),
            pltpu.VMEM((8, 8, NB), F32),
            pltpu.VMEM((8, NB), F32),
            pltpu.VMEM((NB, NB), F32),
            pltpu.VMEM((8, NB), F32),
            pltpu.VMEM((2, TILE, 512), BF16),
            dma((4,)),
            dma((8,)),
            dma((8,)),
            dma((4,)),
            dma((4,)),
            dma((4, 4)),
            dma((8, 2)),
            dma((2,)),
            dma((2,)),
            dma,
            dma((2, 16)),
            dma((2,)),
            dma((8, 2)),
            dma((8,)),
            dma((3, 16)),
            dma((3,)),
            dma((2, 16)),
            dma((2, 4)),
            dma((16,)),
            dma,
            dma((2, 4)),
        ],
        compiler_params=pltpu.CompilerParams(
            collective_id=0, has_side_effects=True, vmem_limit_bytes=56 * 2**20
        ),
    )(matrix, far_diag, vectors, factors)
    updated, far_updated = pl.pallas_call(
        update,
        name="update",
        out_shape=(jax.ShapeDtypeStruct((TILE, TILE), F32), jax.ShapeDtypeStruct((1, TILE), F32)),
        in_specs=[any_spec, any_spec, vmem_spec, vmem_spec],
        out_specs=(any_spec, vmem_spec),
        scratch_shapes=[
            pltpu.VMEM((TILE, TILE), F32),
            pltpu.VMEM((2, TILE, 512), BF16),
            dma,
            dma((TILE // WIDTH,)),
            dma((TILE // WIDTH,)),
        ],
        compiler_params=pltpu.CompilerParams(vmem_limit_bytes=60 * 2**20),
    )(matrix, x, d, far_diag)
    return updated, far_updated


def solution(mesh):
    in_specs = (P("row", "col"), P("row", None), P(("row", "col"), None), P())
    out_specs = (P("row", "col"), P("row", None))
    return jax.shard_map(body, mesh=mesh, in_specs=in_specs, out_specs=out_specs, check_vma=False)
```

```python
import functools

import jax
import jax.numpy as jnp
from jax import lax
from jax.experimental import pallas as pl
from jax.experimental.pallas import tpu as pltpu
from jax.sharding import PartitionSpec as P

TILE = 1536
NB = 128
GRID = 16
HALF = 8
ROWS = 8
LINE = ((2, 0), (2, 1), (1, 1), (3, 1), (1, 0), (3, 0), (0, 1))
COLS = 16
VPIECE = 192
ZPIECE = 96
WIDTH = 512
PEERS = ((0, 0), (0, 1), (1, 0), (0, 3), (3, 0), (1, 1), (3, 3), (1, 3), (3, 1), (0, 2), (2, 0),
         (2, 1), (1, 2), (2, 3), (3, 2), (2, 2))
MESH = pl.DeviceIdType.MESH
F32 = jnp.float32
BF16 = jnp.bfloat16


def dot(left, right):
    return lax.dot_general(left, right, (((1,), (0,)), ((), ())), preferred_element_type=F32)


def dot_exact(left, right, dims=((1,), (0,))):
    return lax.dot_general(
        left, right, (dims, ((), ())), preferred_element_type=F32, precision=lax.Precision.HIGHEST
    )


def halves(value):
    high = value.astype(BF16)
    low = (value - high.astype(F32)).astype(BF16)
    return high, low


def choose(j, values):
    out = jnp.int32(values[0])
    for k, value in enumerate(values):
        if k > 0 and value != values[0]:
            out = jnp.where(j == k, value, out)
    return out


def put(src, dst, send_sem, recv_sem, to_row, to_col, row, col):
    here = jnp.logical_and(to_row == row, to_col == col)

    @pl.when(here)
    def _():
        pltpu.make_async_copy(src, dst, recv_sem).start()

    @pl.when(jnp.logical_not(here))
    def _():
        pltpu.make_async_remote_copy(
            src_ref=src, dst_ref=dst, send_sem=send_sem, recv_sem=recv_sem,
            device_id=(to_row, to_col), device_id_type=MESH,
        ).start()


def sent(src, dst, send_sem, recv_sem, to_row, to_col, row, col):
    here = jnp.logical_and(to_row == row, to_col == col)

    @pl.when(jnp.logical_not(here))
    def _():
        pltpu.make_async_remote_copy(
            src_ref=src, dst_ref=src, send_sem=send_sem, recv_sem=send_sem,
            device_id=(to_row, to_col), device_id_type=MESH,
        ).wait_send()


def arrived(ref, sem):
    pltpu.make_async_copy(ref, ref, sem).wait()


def exchange(
    mat, lowd, vec, fac, x_out, d_out,
    abuf, bhi, blo, vline, vz, vbuf, vcat, vtc, z, zt, parts, lpart, lsend, zsum, zf, vd,
    gpart, g1, g1s, g2, g2s, gf, dmine, xbuf,
    a_sem, vl_send, vl_recv, vz_send, vz_recv, vf_send, vo_send, v_recv, vd_send, vd_recv, r_send, r_recv,
    l_send, l_recv, g_send, g_recv, z_send, z_recv, d_send, d_recv, o_sem,
):
    row = lax.axis_index("row")
    col = lax.axis_index("col")
    diag = row == col
    plain = row != col
    other = jnp.where(col < row, col, jnp.where(diag, GRID - 1 - row, col - row - 1))
    far = GRID - 1 - row
    x, core = row // 2, lax.rem(row, 2)

    sign = 1 - 2 * core

    def peer(j):
        z = lax.rem(col // 4 + sign * choose(j, [p[0] for p in PEERS]) + 4, 4)
        y = lax.rem(lax.rem(col, 4) + sign * choose(j, [p[1] for p in PEERS]) + 4, 4)
        return z * 4 + y

    def line_row(step):
        return lax.rem(x + step[0], 4) * 2 + lax.rem(core + step[1], 2)

    def part_copy(k):
        return pltpu.make_async_copy(
            mat.at[pl.ds(k * 384, 384)], abuf.at[pl.ds(k * 384, 384)], a_sem.at[k]
        )

    for k in range(4):
        part_copy(k).start()

    bar = pltpu.get_barrier_semaphore()

    def greet(j, carry):
        pl.semaphore_signal(
            bar, inc=1, device_id=(row, lax.rem(col + j, COLS)), device_id_type=MESH
        )
        return carry

    lax.fori_loop(1, COLS, greet, 0)
    for step in LINE:
        pl.semaphore_signal(bar, inc=1, device_id=(line_row(step), col), device_id_type=MESH)

    own = pltpu.make_async_copy(vec, vline.at[row], vl_recv.at[row])
    own.start()

    def split_part(k):
        part_copy(k).wait()

        @pl.when(plain)
        def _():
            def split(s, carry):
                rows = pl.ds(pl.multiple_of(k * 384 + s * 32, 32), 32)
                high, low = halves(abuf[rows, :])
                bhi[0, rows, :] = high
                blo[0, rows, :] = low
                return carry

            lax.fori_loop(0, 12, split, 0)

    pl.semaphore_wait(bar, COLS - 1 + ROWS - 1)

    vtile = 2 * row + col // 8
    vpiece = lax.rem(col, 8)
    parity = col // 8
    vlead_row = jnp.where(vtile < HALF, vtile, GRID - 1 - vtile)

    def v_line(j, to_row):
        return pltpu.make_async_remote_copy(
            src_ref=vec, dst_ref=vline.at[row], send_sem=vl_send.at[j],
            recv_sem=vl_recv.at[row], device_id=(to_row, col), device_id_type=MESH,
        )

    def v_line_lead(act):
        @pl.when(vlead_row != row)
        def _():
            act(v_line(7, vlead_row))

    def v_line_each(act):
        for j, step in enumerate(LINE):
            to_row = line_row(step)

            @pl.when(jnp.logical_and(to_row != vlead_row, to_row <= GRID - 1 - vtile))
            def _():
                act(v_line(j, to_row))

    v_line_lead(lambda copy: copy.start())

    lead_near = lax.rem(row, 2) == parity
    lead_src = jnp.where(lead_near, row, far) // 2
    v_rows = pl.ds(vpiece * VPIECE, VPIECE)

    z_at, y_at = col // 4, lax.rem(col, 4)
    z_row = row // 4

    def v_lead_each(act):
        for j, dz in enumerate((0, 1, 3, 2)):
            to_z = lax.rem(z_at + sign * dz + 4, 4)

            @pl.when(jnp.logical_or(to_z == z_row, (to_z < z_row) == lead_near))
            def _():
                act(vline.at[lead_src], vz.at[z_at], vz_send.at[j], vz_recv.at[z_at],
                    row, to_z * 4 + y_at, row, col)

        @pl.when(jnp.logical_not(lead_near))
        def _():
            for k in range(2):
                act(vline.at[lead_src, pl.ds(k * ZPIECE, ZPIECE)], vd, vd_send.at[k], vd_recv,
                    row, 2 * vpiece + k, row, col)

    def v_hand_each(act, before):
        for j, dz in enumerate((0, 1, 3, 2)):
            src = lax.rem(z_at - sign * dz + 4, 4)
            near = lax.rem(row, 2) == src // 2

            @pl.when(jnp.logical_or(z_at == z_row, (z_at < z_row) == near))
            def _():
                before(src)

                for i, dy in enumerate((0, 1, 3, 2)):
                    c = z_at * 4 + lax.rem(y_at + sign * dy + 4, 4)

                    @pl.when(jnp.logical_or(c == row, (c < row) == near))
                    def _():
                        slot = jnp.where(jnp.logical_and(c == row, near), 1, 0)
                        rows = pl.ds((lax.rem(src, 2) * 4 + y_at) * VPIECE, VPIECE)
                        act(vz.at[src], vbuf.at[slot, rows], vf_send.at[j, i], v_recv.at[slot],
                            row, c, row, col)

    def v_other_each(act, before):
        def one(j, carry):
            q = lax.rem(j + vpiece, ROWS)
            steps = ((0, 0),) + LINE
            src = line_row((choose(q, [p[0] for p in steps]), choose(q, [p[1] for p in steps])))
            tile = 2 * src + parity

            @pl.when(jnp.logical_and(tile <= far, src != lead_src))
            def _():
                before(src)

            @pl.when(tile < row)
            def _():
                act(vline.at[src], vbuf.at[1, v_rows], vo_send.at[q, 0], v_recv.at[1],
                    row, tile, row, col)

            @pl.when(tile < far)
            def _():
                act(vline.at[src], vbuf.at[1, v_rows], vo_send.at[q, 1], v_recv.at[1],
                    row, tile + row + 1, row, col)

            return carry

        lax.fori_loop(0, ROWS, one, 0)

    split_part(0)
    arrived(vline.at[lead_src], vl_recv.at[lead_src])
    v_lead_each(put)
    v_line_each(lambda copy: copy.start())
    v_hand_each(put, lambda src: arrived(vz.at[src], vz_recv.at[src]))
    v_other_each(put, lambda src: arrived(vline.at[src], vl_recv.at[src]))

    @pl.when(jnp.logical_and(vtile > far, lead_src != row))
    def _():
        arrived(vline.at[row], vl_recv.at[row])

    split_part(1)
    split_part(2)
    split_part(3)

    @pl.when(diag)
    def _():
        def keep(s, rows, cols, value):
            high, low = halves(value)
            bhi[s, rows, cols] = high
            blo[s, rows, cols] = low

        def block_at(n, carry):
            p, q = n // 6, lax.rem(n, 6)
            rows = pl.ds(pl.multiple_of(p * 256, 256), 256)
            cols = pl.ds(pl.multiple_of(q * 256, 256), 256)

            @pl.when(p != q)
            def _():
                s = jnp.where(p > q, 0, 1)
                block = abuf[rows, cols]
                keep(s, rows, cols, block)
                keep(s, cols, rows, block.T)

            @pl.when(p == q)
            def _():
                block = abuf[rows, cols]
                rr = lax.broadcasted_iota(jnp.int32, (256, 256), 0)
                cc = lax.broadcasted_iota(jnp.int32, (256, 256), 1)
                lower = jnp.where(rr > cc, block, 0.0)
                upper = jnp.where(rr < cc, block, 0.0)
                onto = jnp.where(rr == cc, block, 0.0)
                far_onto = jnp.where(rr == cc, jnp.broadcast_to(lowd[:, cols], (256, 256)), 0.0)
                keep(0, rows, cols, lower + lower.T + onto)
                keep(1, rows, cols, upper + upper.T + far_onto)

            return carry

        lax.fori_loop(0, 36, block_at, 0)

    def cat_v(s):
        for p in range(6):
            at = slice(p * 256, p * 256 + 256)
            high, low = halves(vbuf[s, at, :])
            vcat[s, at, 0:128] = high
            vcat[s, at, 128:256] = low

    def cat_vt(s):
        for p in range(6):
            at = slice(p * 256, p * 256 + 256)
            high, low = halves(vbuf[s, at, :].T)
            vtc[s, 0:128, at] = high
            vtc[s, 128:256, at] = low

    def times(high, low, v):
        full = dot(high, v)
        return full[:, 0:128] + full[:, 128:256] + dot(low, v[:, 0:128])

    def times_t(vt, high, low):
        full = dot(vt, high)
        return full[0:128] + full[128:256] + dot(vt[0:128], low)

    def z_put(s, act=put, half=None):
        def one(j, carry):
            c = peer(j)

            @pl.when(True if half is None else c // 8 == half)
            def _():
                act(z.at[s, pl.ds(c * ZPIECE, ZPIECE)], parts.at[s, col], r_send.at[s, c],
                    r_recv.at[s], row, c, row, col)

            return carry

        lax.fori_loop(0, COLS, one, 0)

    def g_start():
        def one(j, carry):
            c = lax.rem(j + col, COLS)
            put(gpart.at[pl.ds(pl.multiple_of(c * 8, 8), 8)], g1.at[col], g_send.at[0, c],
                g_recv.at[0], row, c, row, col)
            return carry

        lax.fori_loop(0, COLS, one, 0)

    second = jnp.where(diag, 1, 0)
    arrived(vbuf.at[0], v_recv.at[0])
    cat_vt(0)

    def turned_panel(n, carry):
        k = lax.rem(n + z_at // 2, 2)
        at = pl.ds(pl.multiple_of(k * 768, 768), 768)
        part = times_t(vtc[0], bhi[second, :, at], blo[second, :, at])
        zt[:, at] = part
        z[1, at, :] = part.T
        return carry

    lax.fori_loop(0, 2, turned_panel, 0)
    z_put(1)

    arrived(vbuf.at[1], v_recv.at[1])
    cat_v(1)

    @pl.when(plain)
    def _():
        high, low = halves(zt[...])
        y = times(high, low, vcat[1])
        gpart[...] = y + y.T
        g_start()

    def panel(n, carry):
        k = lax.rem(n + z_at // 2, 2)
        rows = pl.ds(pl.multiple_of(k * 768, 768), 768)
        z[0, rows, :] = times(bhi[0, rows, :], blo[0, rows, :], vcat[1])
        z_put(0, half=k)
        return carry

    lax.fori_loop(0, 2, panel, 0)

    @pl.when(diag)
    def _():
        cat_v(0)
        cat_vt(1)
        high, low = halves(zt[...])
        y = times(high, low, vcat[0])
        high, low = halves(z[0])
        full = dot(vtc[1], high)
        gpart[...] = y + full[0:128] + full[128:256] + dot(vtc[1, 0:128, :], low)
        g_start()

    arrived(parts.at[1], r_recv.at[1])
    for step in LINE:
        to = line_row(step)

        @pl.when(to < row)
        def _():
            lsend[to] = parts[1, to] + parts[1, to + row + 1]

    def l_copy(src, to, k):
        return pltpu.make_async_remote_copy(
            src_ref=src, dst_ref=lpart.at[row, k], send_sem=l_send.at[to, k],
            recv_sem=l_recv.at[row], device_id=(to, col), device_id_type=MESH,
        )

    def l_each(act):
        for step in LINE:
            to = line_row(step)

            @pl.when(to < row)
            def _():
                act(l_copy(lsend.at[to], to, 0))

            @pl.when(to > row)
            def _():
                act(l_copy(parts.at[1, to + row + 1], to, 0))
                act(l_copy(parts.at[1, GRID - to + row], to, 1))

    l_each(lambda copy: copy.start())

    arrived(g1, g_recv.at[0])
    g1s[...] = jnp.sum(g1[...], axis=0)

    def g_line(j, carry):
        r = lax.rem(j + row, ROWS)
        put(g1s, g2.at[row], g_send.at[1, r], g_recv.at[1], r, col, row, col)
        return carry

    lax.fori_loop(0, ROWS, g_line, 0)

    arrived(parts.at[0], r_recv.at[0])
    zsum[0] = parts[1, 2 * row + 1]
    zsum[1] = parts[1, row]

    def add_lead(c, carry):
        zsum[jnp.where(c <= row, 0, 1)] += parts[0, c]
        return carry

    lax.fori_loop(0, COLS, add_lead, 0)
    for step in LINE:
        src = line_row(step)

        @pl.when(src < row)
        def _():
            arrived(lpart.at[src], l_recv.at[src])
            zsum[0] += lpart[src, 0]
            zsum[1] += lpart[src, 1]

        @pl.when(src > row)
        def _():
            arrived(lpart.at[src, 0], l_recv.at[src])
            zsum[0] += lpart[src, 0]

    def zf_each(first_j, last_j, act):
        def one(j, carry):
            c = peer(j)
            half = jnp.where(c <= row, 0, 1)
            slot = jnp.where(c == row, 1, 0)
            act(zsum.at[half], zf.at[slot, pl.ds(col * ZPIECE, ZPIECE)], z_send.at[0, j],
                z_recv.at[slot, z_at], row, c, row, col)
            n = lax.rem(j + col, COLS)
            to = lax.rem(row + n, ROWS)
            first = n < ROWS
            half = jnp.where(jnp.logical_or(first, to > row), 0, 1)
            slot = jnp.where(jnp.logical_or(first, to != row), 1, 0)
            to_col = jnp.where(
                first, to + row + 1, jnp.where(to >= row, row, GRID - row + to))
            act(zsum.at[half], zf.at[slot, pl.ds(col * ZPIECE, ZPIECE)], z_send.at[1, j],
                z_recv.at[slot, z_at], to, to_col, row, col)
            return carry

        lax.fori_loop(first_j, last_j, one, 0)

    zf_each(0, 6, put)
    arrived(g2, g_recv.at[1])
    g2s[...] = jnp.sum(g2[...], axis=0)

    def g_row(j, carry):
        c = lax.rem(j + col, COLS)
        put(g2s, gf.at[pl.ds(pl.multiple_of(col * 8, 8), 8)], g_send.at[2, c], g_recv.at[2],
            row, c, row, col)
        return carry

    lax.fori_loop(0, COLS, g_row, 0)
    zf_each(6, COLS, put)

    arrived(gf, g_recv.at[2])
    fac_value = fac[...]
    middle = dot_exact(dot_exact(fac_value, gf[...], ((0,), (0,))), fac_value)

    arrived(vd, vd_recv)
    v_far = vd[...]
    w_far = dot_exact(zsum[1], fac_value) - 0.5 * dot_exact(v_far, middle)
    sums = dot_exact(jnp.ones((8, 128), F32), v_far * w_far, ((1,), (1,)))
    dmine[...] = jnp.concatenate([sums, jnp.zeros((8, 32), F32)], axis=1)

    def d_put(j, carry):
        c = lax.rem(j + col, COLS)
        put(dmine, d_out.at[col], d_send.at[c], d_recv, row, c, row, col)
        return carry

    lax.fori_loop(0, COLS, d_put, 0)

    both = jnp.concatenate([fac_value, -0.5 * middle], axis=0)
    both_high, both_low = halves(both)

    def w_into(step):
        k = lax.rem(z_at + step, 4)

        def one(s, carry):
            rows = pl.ds(pl.multiple_of(k * 384, 384), 384)
            arrived(zf.at[s, rows], z_recv.at[s, k])
            v_high, v_low = halves(vbuf[s, rows, :])
            z_high, z_low = halves(zf[s, rows, :])
            high = jnp.concatenate([z_high, v_high], axis=1)
            low = jnp.concatenate([z_low, v_low], axis=1)
            w = dot(high, both_high) + dot(high, both_low) + dot(low, both_high)
            w_high, w_low = halves(w)
            xbuf[s, rows, :] = jnp.concatenate([v_high, w_high, v_low, w_low], axis=1)
            pltpu.make_async_copy(xbuf.at[s, rows], x_out.at[s, rows], o_sem.at[s, k]).start()
            return carry

        lax.fori_loop(0, 2, one, 0)

    v_line_lead(lambda copy: copy.wait_send())
    v_line_each(lambda copy: copy.wait_send())
    v_lead_each(sent)
    v_hand_each(sent, lambda src: None)
    v_other_each(sent, lambda src: None)
    z_put(0, sent)
    z_put(1, sent)
    l_each(lambda copy: copy.wait_send())

    def row_sent(j, carry):
        sent(g1s, g1s, g_send.at[0, j], None, row, j, row, col)
        sent(g2s, g2s, g_send.at[2, j], None, row, j, row, col)
        return carry

    lax.fori_loop(0, COLS, row_sent, 0)

    def line_sent(j, carry):
        sent(g1s, g1s, g_send.at[1, j], None, j, col, row, col)
        return carry

    lax.fori_loop(0, ROWS, line_sent, 0)

    w_into(0)
    w_into(1)
    w_into(3)
    zf_each(0, COLS, sent)

    def d_sent(j, carry):
        sent(dmine, dmine, d_send.at[j], None, row, j, row, col)
        return carry

    lax.fori_loop(0, COLS, d_sent, 0)
    w_into(2)

    arrived(d_out, d_recv)

    for s in range(2):
        for k in range(4):
            arrived(xbuf.at[s, pl.ds(k * 384, 384)], o_sem.at[s, k])


def update(mat, x_hbm, d, fard, out, far_out, abuf, x, sem, in_sem, out_sem):
    diag = lax.axis_index("row") == lax.axis_index("col")
    x_copy = pltpu.make_async_copy(x_hbm, x, sem)
    x_copy.start()

    def columns(k):
        return pl.ds(pl.multiple_of(k * WIDTH, WIDTH), WIDTH)

    def load(k):
        return pltpu.make_async_copy(mat.at[:, columns(k)], abuf.at[:, columns(k)], in_sem.at[k])

    def store(k):
        return pltpu.make_async_copy(abuf.at[:, columns(k)], out.at[:, columns(k)], out_sem.at[k])

    def each(act):
        def one(k, carry):
            act(k)
            return carry

        lax.fori_loop(0, TILE // WIDTH, one, 0)

    each(lambda k: load(k).start())

    lane = lax.broadcasted_iota(jnp.int32, (128, TILE), 1)
    start = jnp.zeros((128, TILE), jnp.int32)
    for k in range(1, 16):
        start += jnp.where(lane >= k * ZPIECE, ZPIECE, 0)
    pick = jnp.where(lane - start == lax.broadcasted_iota(jnp.int32, (128, TILE), 0), 1.0, 0.0)
    spread = dot_exact(d[:, 0, :], pick)
    piece = lax.broadcasted_iota(jnp.int32, (16, TILE), 0) * ZPIECE
    whole = jnp.sum(jnp.where(piece == start[0:16], spread, 0.0), axis=0, keepdims=True)
    far_out[...] = fard[...] - 2.0 * whole
    x_copy.wait()

    def dot_nt(left, right):
        return lax.dot_general(
            left, right, (((1,), (1,)), ((), ())), preferred_element_type=F32
        )

    def change(s, t, cols, rows=slice(None)):
        v_high, w_high = x[t, cols, 0:128], x[t, cols, 128:256]
        v_low, w_low = x[t, cols, 256:384], x[t, cols, 384:512]
        high = jnp.concatenate([w_high, v_high], axis=1)
        low = jnp.concatenate([w_low, v_low], axis=1)
        left_high, left_low = x[s, rows, 0:256], x[s, rows, 256:512]
        return dot_nt(left_high, high) + dot_nt(left_high, low) + dot_nt(left_low, high)

    @pl.when(jnp.logical_not(diag))
    def _():
        def step(k):
            cols = columns(k)
            load(k).wait()
            abuf[:, cols] -= change(0, 1, cols)
            store(k).start()

        each(step)

    @pl.when(diag)
    def _():
        below = lax.broadcasted_iota(jnp.int32, (WIDTH, WIDTH), 0) >= lax.broadcasted_iota(
            jnp.int32, (WIDTH, WIDTH), 1)
        for k in range(TILE // WIDTH):
            lo, hi = k * WIDTH, k * WIDTH + WIDTH
            cols = slice(lo, hi)
            load(k).wait()
            near = change(1, 1, cols, slice(lo, TILE))
            far = change(0, 0, cols, slice(0, hi))
            if k > 0:
                abuf[0:lo, cols] -= far[0:lo]
            abuf[lo:hi, cols] -= jnp.where(below, near[0:WIDTH], far[lo:hi])
            if hi < TILE:
                abuf[hi:, cols] -= near[WIDTH:]
            store(k).start()

    each(lambda k: store(k).wait())


def body(matrix, far_diag, vectors, factors):
    any_spec = pl.BlockSpec(memory_space=pl.ANY)
    vmem_spec = pl.BlockSpec(memory_space=pltpu.VMEM)
    dma = pltpu.SemaphoreType.DMA
    x, d = pl.pallas_call(
        exchange,
        name="exchange",
        out_shape=(jax.ShapeDtypeStruct((2, TILE, 512), BF16),
                   jax.ShapeDtypeStruct((16, 8, 128), F32)),
        in_specs=[any_spec, vmem_spec, vmem_spec, vmem_spec],
        out_specs=(any_spec, vmem_spec),
        scratch_shapes=[
            pltpu.VMEM((TILE, TILE), F32),
            pltpu.VMEM((2, TILE, TILE), BF16),
            pltpu.VMEM((2, TILE, TILE), BF16),
            pltpu.VMEM((ROWS, VPIECE, NB), F32),
            pltpu.VMEM((4, VPIECE, NB), F32),
            pltpu.VMEM((2, TILE, NB), F32),
            pltpu.VMEM((2, TILE, 2 * NB), BF16),
            pltpu.VMEM((2, 2 * NB, TILE), BF16),
            pltpu.VMEM((2, TILE, NB), F32),
            pltpu.VMEM((NB, TILE), F32),
            pltpu.VMEM((2, COLS, ZPIECE, NB), F32),
            pltpu.VMEM((ROWS, 2, ZPIECE, NB), F32),
            pltpu.VMEM((ROWS, ZPIECE, NB), F32),
            pltpu.VMEM((2, ZPIECE, NB), F32),
            pltpu.VMEM((2, TILE, NB), F32),
            pltpu.VMEM((ZPIECE, NB), F32),
            pltpu.VMEM((NB, NB), F32),
            pltpu.VMEM((16, 8, NB), F32),
            pltpu.VMEM((8, NB), F32),
            pltpu.VMEM((8, 8, NB), F32),
            pltpu.VMEM((8, NB), F32),
            pltpu.VMEM((NB, NB), F32),
            pltpu.VMEM((8, NB), F32),
            pltpu.VMEM((2, TILE, 512), BF16),
            dma((4,)),
            dma((8,)),
            dma((8,)),
            dma((4,)),
            dma((4,)),
            dma((4, 4)),
            dma((8, 2)),
            dma((2,)),
            dma((2,)),
            dma,
            dma((2, 16)),
            dma((2,)),
            dma((8, 2)),
            dma((8,)),
            dma((3, 16)),
            dma((3,)),
            dma((2, 16)),
            dma((2, 4)),
            dma((16,)),
            dma,
            dma((2, 4)),
        ],
        compiler_params=pltpu.CompilerParams(
            collective_id=0, has_side_effects=True, vmem_limit_bytes=56 * 2**20
        ),
    )(matrix, far_diag, vectors, factors)
    updated, far_updated = pl.pallas_call(
        update,
        name="update",
        out_shape=(jax.ShapeDtypeStruct((TILE, TILE), F32), jax.ShapeDtypeStruct((1, TILE), F32)),
        in_specs=[any_spec, any_spec, vmem_spec, vmem_spec],
        out_specs=(any_spec, vmem_spec),
        scratch_shapes=[
            pltpu.VMEM((TILE, TILE), F32),
            pltpu.VMEM((2, TILE, 512), BF16),
            dma,
            dma((TILE // WIDTH,)),
            dma((TILE // WIDTH,)),
        ],
        compiler_params=pltpu.CompilerParams(vmem_limit_bytes=60 * 2**20),
    )(matrix, x, d, far_diag)
    return updated, far_updated


def solution(mesh):
    in_specs = (P("row", "col"), P("row", None), P(("row", "col"), None), P())
    out_specs = (P("row", "col"), P("row", None))
    return jax.shard_map(body, mesh=mesh, in_specs=in_specs, out_specs=out_specs, check_vma=False)
```
